32 devices in a mesh: fsdp: 8 (over y, x, core), seq: 4 (over z).
Axes of the slice: x: 2, y: 2, z: 4, core: 2. Of those that a mesh axis runs over, the one named last changes fastest.
Arguments:
- tokens: bfloat16 [16, 1376, 1024], P('fsdp', 'seq'), may hold values from -24 to 24
- valid_len: int32 [16], P('fsdp'), may hold values from 1204 to 1376, as said below
- cotangent: bfloat16 [16, 1376, 1024], P('fsdp', 'seq'), may hold values from -6 to 6
- norm1_gain: bfloat16 [1024], P('fsdp'), may hold values from 0.59765625 to 1.3984375
- norm1_shift: bfloat16 [1024], P('fsdp'), may hold values from -1 to 1
- qkv_weight: bfloat16 [1024, 3072], P('fsdp'), may hold values from -0.1875 to 0.1875
- query_bias: bfloat16 [1024], P('fsdp'), may hold values from -1.5 to 1.5
- value_bias: bfloat16 [1024], P('fsdp'), may hold values from -0.29882812 to 0.29882812
- proj_weight: bfloat16 [1024, 1024], P('fsdp'), may hold values from -3 to 3
- proj_bias: bfloat16 [1024], P('fsdp'), may hold values from -1 to 1
- attn_scale: bfloat16 [1024], P('fsdp'), may hold values from 0.5 to 1.5
- norm2_gain: bfloat16 [1024], P('fsdp'), may hold values from 0.59765625 to 1.3984375
- norm2_shift: bfloat16 [1024], P('fsdp'), may hold values from -1 to 1
- fc1_weight: bfloat16 [1024, 4096], P('fsdp'), may hold values from -0.1875 to 0.1875
- fc1_bias: bfloat16 [4096], P('fsdp'), may hold values from -1.5 to 1.5
- fc2_weight: bfloat16 [4096, 1024], P('fsdp'), may hold values from -0.125 to 0.125
- fc2_bias: bfloat16 [1024], P('fsdp'), may hold values from -1 to 1
- mlp_scale: bfloat16 [1024], P('fsdp'), may hold values from 0.5 to 1.5
Outputs:
- mixed: bfloat16 [16, 1376, 1024], P('fsdp', 'seq')
- input_grad: float32 [16, 1376, 1024], P('fsdp', 'seq')
- rms_stats: float32 [16, 5], P('fsdp')
- grad_norm1_gain: float32 [1024], P('fsdp')
- grad_norm1_shift: float32 [1024], P('fsdp')
- grad_qkv_weight: float32 [1024, 3072], P('fsdp')
- grad_query_bias: float32 [1024], P('fsdp')
- grad_value_bias: float32 [1024], P('fsdp')
- grad_proj_weight: float32 [1024, 1024], P('fsdp')
- grad_proj_bias: float32 [1024], P('fsdp')
- grad_attn_scale: float32 [1024], P('fsdp')
- grad_norm2_gain: float32 [1024], P('fsdp')
- grad_norm2_shift: float32 [1024], P('fsdp')
- grad_fc1_weight: float32 [1024, 4096], P('fsdp')
- grad_fc1_bias: float32 [4096], P('fsdp')
- grad_fc2_weight: float32 [4096, 1024], P('fsdp')
- grad_fc2_bias: float32 [1024], P('fsdp')
- grad_mlp_scale: float32 [1024], P('fsdp')
The draws below stay inside these ranges and needn't reach their ends.
Inputs may be any that keep to these rules, and one draw needn't show every extreme that they name: Token slots at or above an image's valid_len are padding; some image has 1376 and some has 1204 in every draw.
All inputs are finite; a program needn't handle non-finite values.
Results may differ from the reference program's by a relative error of at most 0.01.
Values may be sent and summed in bfloat16 or wider, within the bound.
A program may use at most 256 MiB of HBM per device.

```python
import math
import jax
import jax.numpy as jnp
from jax import lax

D = 1024
HEADS = 16
FF = 4096
HEAD_DIM = 64
LENGTH = 1376
IMG_DEV = 2
TOK_DEV = 344
IMAGES = 16
N_FSDP = 8


def draw_tokens(key, part):
    key = jax.random.fold_in(key, 5)
    keys_all = jax.random.split(key, 3)
    base = jax.random.normal(keys_all[0], (IMAGES, LENGTH, D), jnp.float32)
    place = jnp.arange(LENGTH, dtype=jnp.float32) / LENGTH
    rough = jnp.exp(jax.random.uniform(keys_all[1], (IMAGES, LENGTH, 1), jnp.float32, 0.0, math.log(10.0))) / 3.0
    columns = jnp.exp(jax.random.uniform(keys_all[2], (1, 1, D), jnp.float32, -0.7, 0.7))
    rise = jnp.exp(place * math.log(3.0)) / 1.5
    values = base * rough * rise[None, :, None] * columns
    return jnp.clip(values, -24.0, 24.0).astype(jnp.bfloat16)


def draw_valid_len(key, part):
    key = jax.random.fold_in(key, 11)
    first_key, second_key = jax.random.split(key)
    most_pad = TOK_DEV // 2
    pads = jax.random.randint(first_key, (IMAGES,), 0, most_pad + 1, dtype=jnp.int32)
    order = jax.random.permutation(second_key, IMAGES)
    pads = pads.at[order[0]].set(0).at[order[1]].set(most_pad)
    return (LENGTH - pads).astype(jnp.int32)


def block_scale(key, extent, cuts, low, top_value):
    def one(axis_at, shards_of):
        heights = jax.random.uniform(jax.random.fold_in(jax.random.fold_in(key, 6), axis_at), (shards_of,), jnp.float32, low / len(cuts), top_value / len(cuts))
        return jnp.repeat(jnp.exp(heights), extent[axis_at] // shards_of).reshape((-1,) + (1,) * (len(extent) - axis_at - 1))

    factor_of = one(*cuts[0])
    for cut in cuts[1:]:
        factor_of = factor_of * one(*cut)
    return factor_of


def scatter_about(key, extent, spread, limit, shards=(), kind=jnp.bfloat16):
    drawn = jax.random.normal(key, extent, jnp.float32) * spread
    if len(shards) > 0:
        drawn = block_scale(key, extent, shards, -0.22, 0.18) * drawn
    return jnp.clip(drawn, min=-limit, max=limit).astype(kind)


def setup_inputs(seed: int = 0) -> dict:
    key_list = jax.random.split(jax.random.key(seed), 19)
    return {
        "tokens": draw_tokens(jax.random.fold_in(key_list[18], 71), 0),
        "valid_len": draw_valid_len(jax.random.fold_in(key_list[18], 71), 0),
        "cotangent": scatter_about(key_list[2], (IMAGES, LENGTH, D), 1.0, 6.0, ((0, 8), (1, 4))),
        "norm1_gain": jnp.clip(0.59765625 + 0.80078125 * jax.random.uniform(key_list[3], (D,), jnp.float32) ** block_scale(key_list[3], (D,), ((0, 8),), -0.2, 0.2), 0.59765625, 1.3984375).astype(jnp.bfloat16),
        "norm1_shift": scatter_about(key_list[4], (D,), 0.2, 1.0, ((0, 8),)),
        "qkv_weight": scatter_about(key_list[5], (D, 3 * D), D ** -0.5, 0.1875, ((0, 8),)),
        "query_bias": scatter_about(key_list[6], (D,), 0.3, 1.5, ((0, 8),)),
        "value_bias": scatter_about(key_list[7], (D,), 0.05, 0.29882812, ((0, 8),)),
        "proj_weight": scatter_about(key_list[8], (D, D), (max(D // 256, 4)) ** -0.5, 3.0, ((0, 8),)),
        "proj_bias": scatter_about(key_list[9], (D,), 0.2, 1.0, ((0, 8),)),
        "attn_scale": jnp.clip(0.5 + 1.0 * jax.random.uniform(key_list[10], (D,), jnp.float32) ** block_scale(key_list[10], (D,), ((0, 8),), -0.2, 0.2), 0.5, 1.5).astype(jnp.bfloat16),
        "norm2_gain": jnp.clip(0.59765625 + 0.80078125 * jax.random.uniform(key_list[11], (D,), jnp.float32) ** block_scale(key_list[11], (D,), ((0, 8),), -0.2, 0.2), 0.59765625, 1.3984375).astype(jnp.bfloat16),
        "norm2_shift": scatter_about(key_list[12], (D,), 0.2, 1.0, ((0, 8),)),
        "fc1_weight": scatter_about(key_list[13], (D, FF), D ** -0.5, 0.1875, ((0, 8),)),
        "fc1_bias": scatter_about(key_list[14], (FF,), 0.3, 1.5, ((0, 8),)),
        "fc2_weight": scatter_about(key_list[15], (FF, D), (FF // 2) ** -0.5, 0.125, ((0, 8),)),
        "fc2_bias": scatter_about(key_list[16], (D,), 0.2, 1.0, ((0, 8),)),
        "mlp_scale": jnp.clip(0.5 + 1.0 * jax.random.uniform(key_list[17], (D,), jnp.float32) ** block_scale(key_list[17], (D,), ((0, 8),), -0.2, 0.2), 0.5, 1.5).astype(jnp.bfloat16),
    }


EPSILON = 1e-06
PRECISE = lax.Precision.HIGHEST

@jax.custom_vjp
def low(v):
    return lax.optimization_barrier(v.astype(jnp.bfloat16)).astype(jnp.float32)

@jax.custom_vjp
def low_back(v):
    return v

def low_keep(v):
    return (low(v), None)

def low_pass(kept, grad):
    return (grad,)

def back_keep(v):
    return (v, None)

def back_low(kept, grad):
    return (low(grad),)
low.defvjp(low_keep, low_pass)
low_back.defvjp(back_keep, back_low)

def layer_norm(values, gain, shift):
    average = lax.optimization_barrier(jnp.mean(values, axis=-1, keepdims=True))
    centered = values - average
    variance = lax.optimization_barrier(jnp.mean(centered * centered, axis=-1, keepdims=True))
    return centered * lax.rsqrt(variance + EPSILON) * gain + shift

def head_attend(inputs_one):
    queries, keys_in, values_in, length_one = inputs_one
    scores = jnp.dot(queries, keys_in.T, precision=PRECISE) * HEAD_DIM ** (-0.5)
    scores = low_back(scores)
    positions = jnp.arange(LENGTH, dtype=jnp.int32)
    scores = jnp.where(positions[None, :] < length_one, scores, -1e+30)
    highest = lax.optimization_barrier(jnp.max(scores, axis=-1, keepdims=True))
    exponent = jnp.exp(scores - highest)
    probabilities = exponent / lax.optimization_barrier(jnp.sum(exponent, axis=-1, keepdims=True))
    return jnp.dot(low(probabilities), values_in, precision=PRECISE)

def forward(tokens_f, lengths, norm1_gain, norm1_shift, qkv_weight, query_bias, value_bias, proj_weight, proj_bias, attn_scale, norm2_gain, norm2_shift, fc1_weight, fc1_bias, fc2_weight, fc2_bias, mlp_scale):
    group = tokens_f.shape[0]
    normed_first = low(layer_norm(tokens_f, norm1_gain, norm1_shift))
    bias_all = jnp.concatenate([query_bias, jnp.zeros((D,), jnp.float32), value_bias])
    projected = jnp.einsum('gtd,de->gte', normed_first, qkv_weight, precision=PRECISE) + bias_all
    projected = low(low_back(projected))
    heads_all = projected.reshape(group, LENGTH, 3, HEADS, HEAD_DIM).transpose(2, 0, 3, 1, 4)
    heads_all = heads_all.reshape(3, group * HEADS, LENGTH, HEAD_DIM)
    lengths_rep = jnp.repeat(lengths, HEADS)
    mixed_heads = lax.map(jax.checkpoint(head_attend), (heads_all[0], heads_all[1], heads_all[2], lengths_rep))
    attended = mixed_heads.reshape(group, HEADS, LENGTH, HEAD_DIM).transpose(0, 2, 1, 3).reshape(group, LENGTH, D)
    attended = low(low_back(attended))
    attn_out = low_back(jnp.einsum('gtd,de->gte', attended, proj_weight, precision=PRECISE) + proj_bias)
    branch_attn = attn_scale * attn_out
    middle = tokens_f + branch_attn
    normed_second = low(layer_norm(middle, norm2_gain, norm2_shift))
    hidden_pre = low_back(jnp.einsum('gtd,df->gtf', normed_second, fc1_weight, precision=PRECISE) + fc1_bias)
    hidden = low(jax.nn.gelu(hidden_pre, approximate=False))
    mlp_out = low_back(jnp.einsum('gtf,fd->gtd', hidden, fc2_weight, precision=PRECISE) + fc2_bias)
    branch_mlp = mlp_scale * mlp_out
    result = middle + branch_mlp
    return (result, (branch_attn, middle, branch_mlp))

def reference(tokens, valid_len, cotangent, norm1_gain, norm1_shift, qkv_weight, query_bias, value_bias, proj_weight, proj_bias, attn_scale, norm2_gain, norm2_shift, fc1_weight, fc1_bias, fc2_weight, fc2_bias, mlp_scale):
    params = tuple((weight_one.astype(jnp.float32) for weight_one in (norm1_gain, norm1_shift, qkv_weight, query_bias, value_bias, proj_weight, proj_bias, attn_scale, norm2_gain, norm2_shift, fc1_weight, fc1_bias, fc2_weight, fc2_bias, mlp_scale)))
    token_groups = tokens.astype(jnp.float32).reshape(N_FSDP, IMG_DEV, LENGTH, D)
    cot_groups = cotangent.astype(jnp.float32).reshape(N_FSDP, IMG_DEV, LENGTH, D)
    length_groups = valid_len.astype(jnp.int32).reshape(N_FSDP, IMG_DEV)

    def group_step(summed, inputs_one):
        tokens_f, cot_f, lengths = inputs_one

        def run(tokens_in, *weights_in):
            return forward(tokens_in, lengths, *weights_in)
        result, pullback, extras = jax.vjp(run, tokens_f, *params, has_aux=True)
        gradients = pullback(cot_f)
        live = (jnp.arange(LENGTH, dtype=jnp.int32)[None, :] < lengths[:, None]).astype(jnp.float32)[:, :, None]
        counted = lengths.astype(jnp.float32) * D
        pieces = (tokens_f, extras[0], extras[1], extras[2], result)
        stats = jnp.stack([jnp.sqrt(lax.optimization_barrier(jnp.sum(live * piece * piece, axis=(1, 2))) / counted) for piece in pieces], axis=-1)
        summed = tuple((before + added for before, added in zip(summed, gradients[1:])))
        return (summed, (result.astype(jnp.bfloat16), gradients[0], stats))
    start = tuple((jnp.zeros(param.shape, jnp.float32) for param in params))
    summed, (results, input_grads, stats) = lax.scan(group_step, start, (token_groups, cot_groups, length_groups))
    return (results.reshape(IMAGES, LENGTH, D), input_grads.reshape(IMAGES, LENGTH, D), stats.reshape(IMAGES, 5), summed[0], summed[1], summed[2], summed[3], summed[4], summed[5], summed[6], summed[7], summed[8], summed[9], summed[10], summed[11], summed[12], summed[13], summed[14])
```

```python
import functools

import jax
import jax.numpy as jnp
from jax import lax
from jax.experimental import pallas as pl
from jax.experimental.pallas import tpu as pltpu
from jax.sharding import PartitionSpec as P

EPSILON = 1e-06
HEAD_DIM = 64


def for_sending(value):
    return jax.tree.map(lambda a: a.astype(jnp.bfloat16) if a.dtype == jnp.float32 else a, value)


def layer_norm(values, gain, shift):
    average = jnp.mean(values, axis=-1, keepdims=True)
    centered = values - average
    variance = jnp.mean(centered * centered, axis=-1, keepdims=True)
    return centered * lax.rsqrt(variance + EPSILON) * gain + shift


def gelu_exact(values):
    return jax.nn.gelu(values, approximate=False)


def block_rows(length):
    return length // 2


def attend_image(inputs_one):
    queries, keys_in, values_in, length_one = inputs_one
    length = queries.shape[0]
    rows = block_rows(length)
    scaling = queries.shape[2] ** (-0.5)
    live_keys = (jnp.arange(length, dtype=jnp.int32) < length_one)[None, None, :]
    outputs = []
    totals = []
    for section in range(length // rows):
        part_q = queries[section * rows : (section + 1) * rows]
        scores = (
            jnp.einsum("qhe,khe->hqk", part_q, keys_in, preferred_element_type=jnp.float32)
            * scaling
        )
        scores = jnp.where(live_keys, scores, -1e30)
        highest = jnp.max(scores, axis=-1, keepdims=True)
        exponent = jnp.exp(scores - highest)
        row_sums = jnp.sum(exponent, axis=-1, keepdims=True)
        probabilities = (exponent / row_sums).astype(jnp.bfloat16)
        outputs.append(
            jnp.einsum("hqk,khe->qhe", probabilities, values_in, preferred_element_type=jnp.float32)
        )
        totals.append(highest + jnp.log(row_sums))
    return (jnp.concatenate(outputs, axis=0).astype(jnp.bfloat16), jnp.concatenate(totals, axis=1))


def attend_back(inputs_one):
    queries, keys_in, values_in, grad_out, log_total, length_one = inputs_one
    length = queries.shape[0]
    rows = block_rows(length)
    scaling = queries.shape[2] ** (-0.5)
    live_keys = (jnp.arange(length, dtype=jnp.int32) < length_one)[None, None, :]
    grad_keys = jnp.zeros(keys_in.shape, jnp.float32)
    grad_values = jnp.zeros(values_in.shape, jnp.float32)
    grad_queries = []
    for section in range(length // rows):
        part_q = queries[section * rows : (section + 1) * rows]
        part_grad = grad_out[section * rows : (section + 1) * rows]
        part_total = log_total[:, section * rows : (section + 1) * rows]
        scores = (
            jnp.einsum("qhe,khe->hqk", part_q, keys_in, preferred_element_type=jnp.float32)
            * scaling
        )
        scores = jnp.where(live_keys, scores, -1e30)
        probabilities = jnp.exp(scores - part_total)
        rounded = probabilities.astype(jnp.bfloat16)
        grad_prob = jnp.einsum(
            "qhe,khe->hqk", part_grad, values_in, preferred_element_type=jnp.float32
        )
        centre = jnp.sum(probabilities * grad_prob, axis=-1, keepdims=True)
        grad_scores = (probabilities * (grad_prob - centre)).astype(jnp.bfloat16)
        grad_queries.append(
            jnp.einsum("hqk,khe->qhe", grad_scores, keys_in, preferred_element_type=jnp.float32)
            * scaling
        )
        grad_keys = (
            grad_keys
            + jnp.einsum("hqk,qhe->khe", grad_scores, part_q, preferred_element_type=jnp.float32)
            * scaling
        )
        grad_values = grad_values + jnp.einsum(
            "hqk,qhe->khe", rounded, part_grad, preferred_element_type=jnp.float32
        )
    stacked = jnp.stack([jnp.concatenate(grad_queries, axis=0), grad_keys, grad_values], axis=1)
    return stacked.astype(jnp.bfloat16)


def generic_device(
    tokens,
    valid_len,
    cotangent,
    norm1_gain,
    norm1_shift,
    qkv_weight,
    query_bias,
    value_bias,
    proj_weight,
    proj_bias,
    attn_scale,
    norm2_gain,
    norm2_shift,
    fc1_weight,
    fc1_bias,
    fc2_weight,
    fc2_bias,
    mlp_scale,
):
    gathered = (
        lax.all_gather(norm1_gain, "fsdp", axis=0, tiled=True),
        lax.all_gather(norm1_shift, "fsdp", axis=0, tiled=True),
        lax.all_gather(qkv_weight, "fsdp", axis=0, tiled=True),
        lax.all_gather(query_bias, "fsdp", axis=0, tiled=True),
        lax.all_gather(value_bias, "fsdp", axis=0, tiled=True),
        lax.all_gather(proj_weight, "fsdp", axis=0, tiled=True),
        lax.all_gather(proj_bias, "fsdp", axis=0, tiled=True),
        lax.all_gather(attn_scale, "fsdp", axis=0, tiled=True),
        lax.all_gather(norm2_gain, "fsdp", axis=0, tiled=True),
        lax.all_gather(norm2_shift, "fsdp", axis=0, tiled=True),
        lax.all_gather(fc1_weight, "fsdp", axis=0, tiled=True),
        lax.all_gather(fc1_bias, "fsdp", axis=0, tiled=True),
        lax.all_gather(fc2_weight, "fsdp", axis=0, tiled=True),
        lax.all_gather(fc2_bias, "fsdp", axis=0, tiled=True),
        lax.all_gather(mlp_scale, "fsdp", axis=0, tiled=True),
    )
    (
        gain_one,
        shift_one,
        weight_qkv,
        bias_query,
        bias_value,
        weight_proj,
        bias_proj,
        scale_one,
        gain_two,
        shift_two,
        weight_up,
        bias_up,
        weight_down,
        bias_down,
        scale_two,
    ) = gathered
    images_here, tok_here, width = tokens.shape
    seq_count = lax.axis_size("seq")
    head_cols = width // seq_count
    heads_here = head_cols // HEAD_DIM
    length = tok_here * seq_count
    inputs_f = tokens.astype(jnp.float32)
    gain_first = gain_one.astype(jnp.float32)
    shift_first = shift_one.astype(jnp.float32)
    gain_second = gain_two.astype(jnp.float32)
    shift_second = shift_two.astype(jnp.float32)
    scale_first = scale_one.astype(jnp.float32)
    scale_second = scale_two.astype(jnp.float32)
    normed_first = layer_norm(inputs_f, gain_first, shift_first).astype(jnp.bfloat16)
    bias_all = jnp.concatenate(
        [
            bias_query.astype(jnp.float32),
            jnp.zeros((width,), jnp.float32),
            bias_value.astype(jnp.float32),
        ]
    )
    projected = (
        jnp.einsum("mtd,de->mte", normed_first, weight_qkv, preferred_element_type=jnp.float32)
        + bias_all
    ).astype(jnp.bfloat16)
    by_heads = lax.all_to_all(
        projected.reshape(images_here, tok_here, 3, seq_count, head_cols),
        "seq",
        split_axis=3,
        concat_axis=1,
        tiled=True,
    )
    by_heads = by_heads.reshape(images_here, length, 3, heads_here, HEAD_DIM)
    attended, log_total = lax.map(
        attend_image, (by_heads[:, :, 0], by_heads[:, :, 1], by_heads[:, :, 2], valid_len)
    )
    attended_tok = lax.all_to_all(
        for_sending(attended.reshape(images_here, length, 1, head_cols)),
        "seq",
        split_axis=1,
        concat_axis=2,
        tiled=True,
    )
    attended_tok = attended_tok.reshape(images_here, tok_here, width)
    attn_out = jnp.einsum(
        "mtd,de->mte", attended_tok, weight_proj, preferred_element_type=jnp.float32
    ) + bias_proj.astype(jnp.float32)
    branch_attn = scale_first * attn_out
    middle = inputs_f + branch_attn
    normed_second = layer_norm(middle, gain_second, shift_second).astype(jnp.bfloat16)
    hidden_pre = jnp.einsum(
        "mtd,df->mtf", normed_second, weight_up, preferred_element_type=jnp.float32
    ) + bias_up.astype(jnp.float32)
    hidden = gelu_exact(hidden_pre).astype(jnp.bfloat16)
    mlp_out = jnp.einsum(
        "mtf,fd->mtd", hidden, weight_down, preferred_element_type=jnp.float32
    ) + bias_down.astype(jnp.float32)
    branch_mlp = scale_second * mlp_out
    result = middle + branch_mlp
    positions = lax.axis_index("seq") * tok_here + jnp.arange(tok_here, dtype=jnp.int32)
    live = (positions[None, :] < valid_len[:, None]).astype(jnp.float32)[:, :, None]
    squares = jnp.stack(
        [
            jnp.sum(live * piece * piece, axis=(1, 2))
            for piece in (inputs_f, branch_attn, middle, branch_mlp, result)
        ],
        axis=-1,
    )
    squares = lax.psum(squares, "seq")
    rms_stats = jnp.sqrt(squares / (valid_len.astype(jnp.float32)[:, None] * width))
    grad_result = cotangent.astype(jnp.float32)
    grad_mlp_scale = jnp.sum(grad_result * mlp_out, axis=(0, 1))
    grad_mlp_out = (grad_result * scale_second).astype(jnp.bfloat16)
    grad_fc2_bias = jnp.sum(grad_mlp_out, axis=(0, 1), dtype=jnp.float32)
    grad_fc2_weight = jnp.einsum(
        "mtf,mtd->fd", hidden, grad_mlp_out, preferred_element_type=jnp.float32
    )
    grad_hidden = jnp.einsum(
        "mtd,fd->mtf", grad_mlp_out, weight_down, preferred_element_type=jnp.float32
    )
    gelu_value, gelu_back = jax.vjp(gelu_exact, hidden_pre)
    grad_pre = gelu_back(grad_hidden)[0].astype(jnp.bfloat16)
    grad_fc1_bias = jnp.sum(grad_pre, axis=(0, 1), dtype=jnp.float32)
    grad_fc1_weight = jnp.einsum(
        "mtd,mtf->df", normed_second, grad_pre, preferred_element_type=jnp.float32
    )
    grad_normed_second = jnp.einsum(
        "mtf,df->mtd", grad_pre, weight_up, preferred_element_type=jnp.float32
    )
    norm_value, norm_back = jax.vjp(layer_norm, middle, gain_second, shift_second)
    grad_middle_norm, grad_norm2_gain, grad_norm2_shift = norm_back(grad_normed_second)
    grad_middle = grad_result + grad_middle_norm
    grad_attn_scale = jnp.sum(grad_middle * attn_out, axis=(0, 1))
    grad_attn_out = (grad_middle * scale_first).astype(jnp.bfloat16)
    grad_proj_bias = jnp.sum(grad_attn_out, axis=(0, 1), dtype=jnp.float32)
    grad_proj_weight = jnp.einsum(
        "mtd,mte->de", attended_tok, grad_attn_out, preferred_element_type=jnp.float32
    )
    grad_attended = jnp.einsum(
        "mte,de->mtd", grad_attn_out, weight_proj, preferred_element_type=jnp.float32
    ).astype(jnp.bfloat16)
    grad_heads = lax.all_to_all(
        grad_attended.reshape(images_here, tok_here, seq_count, head_cols),
        "seq",
        split_axis=2,
        concat_axis=1,
        tiled=True,
    )
    grad_heads = grad_heads.reshape(images_here, length, heads_here, HEAD_DIM)
    grad_qkv = lax.map(
        attend_back,
        (by_heads[:, :, 0], by_heads[:, :, 1], by_heads[:, :, 2], grad_heads, log_total, valid_len),
    )
    grad_projected = lax.all_to_all(
        for_sending(grad_qkv.reshape(images_here, length, 3, 1, head_cols)),
        "seq",
        split_axis=1,
        concat_axis=3,
        tiled=True,
    )
    grad_projected = grad_projected.reshape(images_here, tok_here, 3 * width)
    grad_query_bias = jnp.sum(grad_projected[:, :, :width], axis=(0, 1), dtype=jnp.float32)
    grad_value_bias = jnp.sum(grad_projected[:, :, 2 * width :], axis=(0, 1), dtype=jnp.float32)
    grad_qkv_weight = jnp.einsum(
        "mtd,mte->de", normed_first, grad_projected, preferred_element_type=jnp.float32
    )
    grad_normed_first = jnp.einsum(
        "mte,de->mtd", grad_projected, weight_qkv, preferred_element_type=jnp.float32
    )
    first_value, first_back = jax.vjp(layer_norm, inputs_f, gain_first, shift_first)
    grad_input_norm, grad_norm1_gain, grad_norm1_shift = first_back(grad_normed_first)
    input_grad = grad_middle + grad_input_norm
    reduced = (
        lax.psum_scatter(grad_norm1_gain, "fsdp", scatter_dimension=0, tiled=True),
        lax.psum_scatter(grad_norm1_shift, "fsdp", scatter_dimension=0, tiled=True),
        lax.psum_scatter(grad_qkv_weight, "fsdp", scatter_dimension=0, tiled=True),
        lax.psum_scatter(grad_query_bias, "fsdp", scatter_dimension=0, tiled=True),
        lax.psum_scatter(grad_value_bias, "fsdp", scatter_dimension=0, tiled=True),
        lax.psum_scatter(grad_proj_weight, "fsdp", scatter_dimension=0, tiled=True),
        lax.psum_scatter(grad_proj_bias, "fsdp", scatter_dimension=0, tiled=True),
        lax.psum_scatter(grad_attn_scale, "fsdp", scatter_dimension=0, tiled=True),
        lax.psum_scatter(grad_norm2_gain, "fsdp", scatter_dimension=0, tiled=True),
        lax.psum_scatter(grad_norm2_shift, "fsdp", scatter_dimension=0, tiled=True),
        lax.psum_scatter(grad_fc1_weight, "fsdp", scatter_dimension=0, tiled=True),
        lax.psum_scatter(grad_fc1_bias, "fsdp", scatter_dimension=0, tiled=True),
        lax.psum_scatter(grad_fc2_weight, "fsdp", scatter_dimension=0, tiled=True),
        lax.psum_scatter(grad_fc2_bias, "fsdp", scatter_dimension=0, tiled=True),
        lax.psum_scatter(grad_mlp_scale, "fsdp", scatter_dimension=0, tiled=True),
    )
    reduced = lax.psum(
        (
            reduced[0],
            reduced[1],
            reduced[2],
            reduced[3],
            reduced[4],
            reduced[5],
            reduced[6],
            reduced[7],
            reduced[8],
            reduced[9],
            reduced[10],
            reduced[11],
            reduced[12],
            reduced[13],
            reduced[14],
        ),
        "seq",
    )
    return (
        result.astype(jnp.bfloat16),
        input_grad,
        rms_stats,
        reduced[0],
        reduced[1],
        reduced[2],
        reduced[3],
        reduced[4],
        reduced[5],
        reduced[6],
        reduced[7],
        reduced[8],
        reduced[9],
        reduced[10],
        reduced[11],
        reduced[12],
        reduced[13],
        reduced[14],
    )


NT = (((1,), (1,)), ((), ()))
NN = (((1,), (0,)), ((), ()))
TN = (((0,), (0,)), ((), ()))

def dotf(a, b, dims):
    return lax.dot_general(a, b, dims, preferred_element_type=jnp.float32)

def att_fwd_kernel(blocks, q_ref, ko_ref, kp_ref, vo_ref, vp_ref, bias_ref, o_ref, st_ref, kbuf, vbuf):
    rows = q_ref.shape[0]
    kbuf[:rows, :128] = ko_ref[...]
    kbuf[rows:, :128] = kp_ref[...]
    vbuf[:rows, :128] = vo_ref[...]
    vbuf[rows:, :128] = vp_ref[...]

    @pl.when(pl.program_id(0) == 0)
    def _():
        kbuf[:, 128:] = bias_ref[...]
        vbuf[:, 128:] = jnp.ones_like(vbuf[:, 128:])

    start = 0
    for size in blocks:
        lane = lax.broadcasted_iota(jnp.int32, (size, 128), 1)
        low = lane < 64
        first = (lane == 0).astype(jnp.bfloat16)
        q = q_ref[start:start + size, :]
        heads = []
        for h in range(2):
            keep = low if h == 0 else jnp.logical_not(low)
            qm = jnp.where(keep, q, jnp.zeros_like(q))
            qx = jnp.concatenate([qm, first], axis=1)
            s = dotf(qx, kbuf[...], NT)
            m = jnp.max(s, axis=-1, keepdims=True)
            p = jnp.exp(s - m).astype(jnp.bfloat16)
            ol = dotf(p, vbuf[...], NN)
            l = ol[:, 128:]
            heads.append(ol[:, :128] / l)
            total = -(m + jnp.log(l))
            hi = total.astype(jnp.bfloat16).astype(jnp.float32)
            mid = (total - hi).astype(jnp.bfloat16).astype(jnp.float32)
            lo = total - hi - mid
            piece = jnp.where(lane == 0, 1.0, jnp.where(lane == 1, hi, jnp.where(lane == 2, mid, jnp.where(lane == 3, lo, 0.0))))
            st_ref[h, start:start + size, :] = piece.astype(jnp.bfloat16)
        o_ref[start:start + size, :] = jnp.where(low, heads[0], heads[1]).astype(jnp.bfloat16)
        start += size

def att_fwd(q, kv_own, kv_other, bias, blocks):
    rows, width = q.shape
    pairs = width // 128
    heads = width // 64
    return pl.pallas_call(
        functools.partial(att_fwd_kernel, blocks),
        grid=(pairs,),
        in_specs=[
            pl.BlockSpec((rows, 128), lambda i: (0, i)),
            pl.BlockSpec((rows, 128), lambda i: (0, i)),
            pl.BlockSpec((rows, 128), lambda i: (0, i)),
            pl.BlockSpec((rows, 128), lambda i: (0, i + pairs)),
            pl.BlockSpec((rows, 128), lambda i: (0, i + pairs)),
            pl.BlockSpec((2 * rows, 128), lambda i: (0, 0)),
        ],
        out_specs=[
            pl.BlockSpec((rows, 128), lambda i: (0, i)),
            pl.BlockSpec((2, rows, 128), lambda i: (i, 0, 0)),
        ],
        out_shape=[
            jax.ShapeDtypeStruct((rows, width), jnp.bfloat16),
            jax.ShapeDtypeStruct((heads, rows, 128), jnp.bfloat16),
        ],
        scratch_shapes=[pltpu.VMEM((2 * rows, 256), jnp.bfloat16), pltpu.VMEM((2 * rows, 256), jnp.bfloat16)],
        compiler_params=pltpu.CompilerParams(vmem_limit_bytes=56 * 2**20),
        name="att_fwd",
    )(q, kv_own, kv_other, kv_own, kv_other, bias)

def att_bwd_kernel(blocks, q_ref, ko_ref, kp_ref, vo_ref, vp_ref, bias_ref, st_ref, do_ref, o_ref, dq_ref, dko_ref, dkp_ref, dvo_ref, dvp_ref, kbuf, vbuf, qx, dox, dkv):
    rows = q_ref.shape[0]
    kbuf[:rows, :128] = ko_ref[...]
    kbuf[rows:, :128] = kp_ref[...]
    vbuf[:rows, :128] = vo_ref[...]
    vbuf[rows:, :128] = vp_ref[...]

    @pl.when(pl.program_id(0) == 0)
    def _():
        kbuf[:, 128:] = bias_ref[...]
        lane = lax.broadcasted_iota(jnp.int32, (2 * rows, 128), 1)
        vbuf[:, 128:] = (lane < 3).astype(jnp.bfloat16)

    lane = lax.broadcasted_iota(jnp.int32, (rows, 128), 1)
    low = lane < 64
    q = q_ref[...]
    do = do_ref[...]
    prod = do.astype(jnp.float32) * o_ref[...].astype(jnp.float32)
    for h in range(2):
        keep = low if h == 0 else jnp.logical_not(low)
        qx[h, :, :128] = jnp.where(keep, q, jnp.zeros_like(q))
        qx[h, :, 128:] = st_ref[h]
        dox[h, :, :128] = jnp.where(keep, do, jnp.zeros_like(do))
        total = -jnp.sum(jnp.where(keep, prod, 0.0), axis=-1, keepdims=True)
        hi = total.astype(jnp.bfloat16).astype(jnp.float32)
        mid = (total - hi).astype(jnp.bfloat16).astype(jnp.float32)
        lo = total - hi - mid
        piece = jnp.where(lane == 0, hi, jnp.where(lane == 1, mid, jnp.where(lane == 2, lo, 0.0)))
        dox[h, :, 128:] = piece.astype(jnp.bfloat16)
    start = 0
    dqs = [None, None]
    for size in blocks:
        dk = None
        dv = None
        kb = kbuf[start:start + size, :]
        vb = vbuf[start:start + size, :]
        for h in range(2):
            s = dotf(kb, qx[h], NT)
            dp = dotf(vb, dox[h], NT)
            p = jnp.exp(s)
            ds = (p * dp).astype(jnp.bfloat16)
            pl_ = p.astype(jnp.bfloat16)
            dv_h = dotf(pl_, dox[h, :, :128], NN)
            dk_h = dotf(ds, qx[h, :, :128], NN)
            dv = dv_h if dv is None else dv + dv_h
            dk = dk_h if dk is None else dk + dk_h
            dq_h = dotf(kb[:, :128], ds, TN)
            dqs[h] = dq_h if dqs[h] is None else dqs[h] + dq_h
        dkv[0, start:start + size, :] = dk.astype(jnp.bfloat16)
        dkv[1, start:start + size, :] = dv.astype(jnp.bfloat16)
        start += size
    dqs = [d.T for d in dqs]
    dq_ref[...] = (jnp.where(low, dqs[0], dqs[1]) * 0.125).astype(jnp.bfloat16)
    dko_ref[...] = dkv[0, :rows, :]
    dkp_ref[...] = dkv[0, rows:, :]
    dvo_ref[...] = dkv[1, :rows, :]
    dvp_ref[...] = dkv[1, rows:, :]

def att_bwd(q, kv_own, kv_other, bias, st, do, o, blocks):
    rows, width = q.shape
    pairs = width // 128
    blk = pl.BlockSpec((rows, 128), lambda i: (0, i))
    blk2 = pl.BlockSpec((rows, 128), lambda i: (0, i + pairs))
    sd = jax.ShapeDtypeStruct((rows, width), jnp.bfloat16)
    return pl.pallas_call(
        functools.partial(att_bwd_kernel, blocks),
        grid=(pairs,),
        in_specs=[blk, blk, blk, blk2, blk2,
            pl.BlockSpec((2 * rows, 128), lambda i: (0, 0)),
            pl.BlockSpec((2, rows, 128), lambda i: (i, 0, 0)), blk, blk],
        out_specs=[blk] * 5,
        out_shape=[sd] * 5,
        scratch_shapes=[pltpu.VMEM((2 * rows, 256), jnp.bfloat16), pltpu.VMEM((2 * rows, 256), jnp.bfloat16),
            pltpu.VMEM((2, rows, 256), jnp.bfloat16), pltpu.VMEM((2, rows, 256), jnp.bfloat16), pltpu.VMEM((2, 2 * rows, 128), jnp.bfloat16)],
        compiler_params=pltpu.CompilerParams(vmem_limit_bytes=56 * 2**20),
        name="att_bwd",
    )(q, kv_own, kv_other, kv_own, kv_other, bias, st, do, o)


F32 = jnp.float32
BF = jnp.bfloat16

def norm_parts(v):
    mean = jnp.mean(v, axis=-1, keepdims=True)
    cen = v - mean
    var = jnp.mean(cen * cen, axis=-1, keepdims=True)
    r = lax.rsqrt(var + EPSILON)
    return cen * r, r

def norm_back(z, r, grad, gain):
    e = grad * gain
    return r * (e - jnp.mean(e, axis=-1, keepdims=True) - z * jnp.mean(e * z, axis=-1, keepdims=True))

def mlp_kernel(att_ref, x_ref, cot_ref, live_ref, vec_ref, wp_ref, w1_ref, b1_ref, w2_ref,
               mixed_ref, gmid_ref, gatt_ref, dwp_ref, dw1_ref, dw2_ref, small_ref, gb1_ref,
               ao, n2, n2t, gm, acc, gn2):
    step = pl.program_id(0)
    last = pl.num_programs(0) - 1

    @pl.when(step == 0)
    def _():
        a = dotf(att_ref[...], wp_ref[...], NN) + vec_ref[0:1, :]
        ao[...] = a
        mid = x_ref[...].astype(F32) + vec_ref[1:2, :] * a
        gmid_ref[...] = mid
        z, _r = norm_parts(mid)
        n = (z * vec_ref[2:3, :] + vec_ref[3:4, :]).astype(BF)
        n2[...] = n
        n2t[...] = n.T
        gm[...] = (cot_ref[...].astype(F32) * vec_ref[5:6, :]).astype(BF)
        acc[...] = jnp.broadcast_to(vec_ref[4:5, :], acc.shape)
        gn2[...] = jnp.zeros_like(gn2)

    u = dotf(n2[...], w1_ref[...], NN) + b1_ref[...]
    phi = 0.5 + 0.5 * lax.erf(u * 0.7071067811865476)
    hid = (u * phi).astype(BF)
    slope = phi + u * jnp.exp(u * u * -0.5) * 0.3989422804014327
    gh = dotf(gm[...], w2_ref[...], NT)
    gpf = gh * slope
    gp = gpf.astype(BF)
    gb1_ref[...] = jnp.sum(gp.astype(F32), axis=0, keepdims=True)
    acc[...] += dotf(hid, w2_ref[...], NN)
    gn2[...] += dotf(gp, w1_ref[...], NT)
    dw2_ref[...] = dotf(hid, gm[...], TN).astype(BF)
    dw1_ref[...] = dotf(n2t[...], gp, NN).astype(BF)

    @pl.when(step == last)
    def _():
        out = acc[...]
        cot = cot_ref[...].astype(F32)
        live = live_ref[...]
        x = x_ref[...].astype(F32)
        mid = gmid_ref[...]
        branch = vec_ref[5:6, :] * out
        res = mid + branch
        mixed_ref[...] = res.astype(BF)
        col = lambda v: jnp.sum(v, axis=0, keepdims=True)
        small_ref[0:1, :] = col(cot * out)
        small_ref[1:2, :] = col(gm[...].astype(F32))
        small_ref[8:9, :] = col(live * x * x)
        ba = vec_ref[1:2, :] * ao[...]
        small_ref[9:10, :] = col(live * ba * ba)
        small_ref[10:11, :] = col(live * mid * mid)
        small_ref[11:12, :] = col(live * branch * branch)
        small_ref[12:13, :] = col(live * res * res)
        z, r = norm_parts(mid)
        g = gn2[...]
        small_ref[2:3, :] = col(g * z)
        small_ref[3:4, :] = col(g)
        gmid = cot + norm_back(z, r, g, vec_ref[2:3, :])
        gmid_ref[...] = gmid
        small_ref[4:5, :] = col(gmid * ao[...])
        gao = (gmid * vec_ref[1:2, :]).astype(BF)
        small_ref[5:6, :] = col(gao.astype(F32))
        gatt_ref[...] = dotf(gao, wp_ref[...], NT).astype(BF)
        dwp_ref[...] = dotf(att_ref[...], gao, TN).astype(BF)

def mlp(att, x, cot, live, vec, wp, w1, b1, w2, fc=512):
    rows, width = att.shape
    ff = w1.shape[1]
    full = lambda s: pl.BlockSpec(s, lambda j: (0,) * len(s))
    sd = jax.ShapeDtypeStruct
    return pl.pallas_call(
        mlp_kernel, grid=(ff // fc,),
        in_specs=[full((rows, width)), full((rows, width)), full((rows, width)), full((rows, 1)), full((8, width)), full((width, width)),
            pl.BlockSpec((width, fc), lambda j: (0, j)), pl.BlockSpec((1, fc), lambda j: (0, j)), pl.BlockSpec((fc, width), lambda j: (j, 0))],
        out_specs=[full((rows, width)), full((rows, width)), full((rows, width)), full((width, width)),
            pl.BlockSpec((width, fc), lambda j: (0, j)), pl.BlockSpec((fc, width), lambda j: (j, 0)), full((16, width)), pl.BlockSpec((1, fc), lambda j: (0, j))],
        out_shape=[sd((rows, width), BF), sd((rows, width), F32), sd((rows, width), BF), sd((width, width), BF), sd((width, ff), BF), sd((ff, width), BF), sd((16, width), F32), sd((1, ff), F32)],
        scratch_shapes=[pltpu.VMEM((rows, width), F32), pltpu.VMEM((rows, width), BF), pltpu.VMEM((width, rows), BF), pltpu.VMEM((rows, width), BF), pltpu.VMEM((rows, width), F32), pltpu.VMEM((rows, width), F32)],
        compiler_params=pltpu.CompilerParams(vmem_limit_bytes=60 * 2**20), name="mlp",
    )(att, x, cot, live, vec, wp, w1, b1, w2)

def qkv_kernel(x_ref, vec_ref, w_ref, b_ref, n_ref, q_ref, kv_ref, n1):
    step = pl.program_id(0)
    @pl.when(step == 0)
    def _():
        z, _r = norm_parts(x_ref[...].astype(F32))
        n = (z * vec_ref[0:1, :] + vec_ref[1:2, :]).astype(BF)
        n1[...] = n
        n_ref[...] = n
    w = w_ref.shape[1]
    y = (dotf(n1[...], w_ref[...], NN) + b_ref[...]).astype(BF)
    @pl.when(step == 2)
    def _():
        q_ref[...] = y * jnp.asarray(0.125, BF)
    @pl.when(step != 2)
    def _():
        kv_ref[...] = y

def qkv(x, vec, w, b):
    rows, width = x.shape
    full = lambda s: pl.BlockSpec(s, lambda j: (0,) * len(s))
    sd = jax.ShapeDtypeStruct
    rot = lambda j: (0, (j + 1) % 3)
    return pl.pallas_call(qkv_kernel, grid=(3,),
        in_specs=[full((rows, width)), full((8, width)), pl.BlockSpec((width, width), rot), pl.BlockSpec((1, width), rot)],
        out_specs=[full((rows, width)), full((rows, width)), pl.BlockSpec((rows, width), lambda j: (0, jnp.minimum(j, 1)))],
        out_shape=[sd((rows, width), BF), sd((rows, width), BF), sd((rows, 2 * width), BF)],
        scratch_shapes=[pltpu.VMEM((rows, width), BF)],
        compiler_params=pltpu.CompilerParams(vmem_limit_bytes=56 * 2**20), name="qkv")(x, vec, w, b)

def qback_kernel(dq_ref, dko_ref, dvo_ref, dkr_ref, dvr_ref, x_ref, n_ref, gmid_ref, vec_ref, w_ref, dw_ref, gx_ref, small_ref, nt, gn):
    step = pl.program_id(0)
    @pl.when(step == 0)
    def _():
        nt[...] = n_ref[...].T
        gn[...] = jnp.zeros_like(gn)
    def do(y):
        dw_ref[...] = dotf(nt[...], y, NN).astype(BF)
        gn[...] += dotf(y, w_ref[...], NT)
        return jnp.sum(y.astype(F32), axis=0, keepdims=True)
    @pl.when(step == 0)
    def _():
        small_ref[0:1, :] = do(dq_ref[...])
    @pl.when(step == 1)
    def _():
        do((dko_ref[...].astype(F32) + dkr_ref[...].astype(F32)).astype(BF))
    @pl.when(step == 2)
    def _():
        small_ref[1:2, :] = do((dvo_ref[...].astype(F32) + dvr_ref[...].astype(F32)).astype(BF))
        z, r = norm_parts(x_ref[...].astype(F32))
        g = gn[...]
        small_ref[2:3, :] = jnp.sum(g * z, axis=0, keepdims=True)
        small_ref[3:4, :] = jnp.sum(g, axis=0, keepdims=True)
        gx_ref[...] = (gmid_ref[...] + norm_back(z, r, g, vec_ref[0:1, :])).astype(BF)

def qback(dq, dko, dvo, dkr, dvr, x, n, gmid, vec, w):
    rows, width = x.shape
    full = lambda s: pl.BlockSpec(s, lambda j: (0,) * len(s))
    sd = jax.ShapeDtypeStruct
    f = full((rows, width))
    return pl.pallas_call(qback_kernel, grid=(3,),
        in_specs=[f] * 8 + [full((8, width)), pl.BlockSpec((width, width), lambda j: (0, j))],
        out_specs=[pl.BlockSpec((width, width), lambda j: (0, j)), f, full((8, width))],
        out_shape=[sd((width, 3 * width), BF), sd((rows, width), BF), sd((8, width), F32)],
        scratch_shapes=[pltpu.VMEM((width, rows), BF), pltpu.VMEM((rows, width), F32)],
        compiler_params=pltpu.CompilerParams(vmem_limit_bytes=60 * 2**20), name="qback")(dq, dko, dvo, dkr, dvr, x, n, gmid, vec, w)


def relayout_pairs(groups, seq_count, turn):
    half = seq_count // 2
    pairs = []
    for f in range(groups):
        for z in range(seq_count):
            image = (z + turn) % half
            target = (f // 2 * 2 + z // half, f % 2 * half + image)
            pairs.append((f * seq_count + z, target[0] * seq_count + target[1]))
    return pairs


AXES = ("fsdp", "seq")


def fast_device(
    tokens,
    valid_len,
    cotangent,
    norm1_gain,
    norm1_shift,
    qkv_weight,
    query_bias,
    value_bias,
    proj_weight,
    proj_bias,
    attn_scale,
    norm2_gain,
    norm2_shift,
    fc1_weight,
    fc1_bias,
    fc2_weight,
    fc2_bias,
    mlp_scale,
):
    groups = lax.axis_size("fsdp")
    seq_count = lax.axis_size("seq")
    images_here, tok_here, width = tokens.shape
    rows = 2 * tok_here
    place = lax.axis_index("seq")
    group = lax.axis_index("fsdp")
    core = group % 2
    turns = range(2)
    pairs = [relayout_pairs(groups, seq_count, turn) for turn in turns]
    back = [[(b, a) for a, b in pair] for pair in pairs]
    swap = [(f, f ^ 1) for f in range(groups)]

    def spread(block):
        parts = []
        for turn in turns:
            sent = lax.dynamic_index_in_dim(block, (place + turn) % 2, 0, keepdims=False)
            parts.append(lax.ppermute(sent, AXES, pairs[turn]))
        return jnp.concatenate(parts, axis=0)

    def collect(block):
        got = [lax.ppermute(block[turn * tok_here : (turn + 1) * tok_here], AXES, back[turn]) for turn in turns]
        even = place % 2 == 0
        return jnp.stack([jnp.where(even, got[0], got[1]), jnp.where(even, got[1], got[0])])

    small = jnp.concatenate(
        [
            norm1_gain, norm1_shift, query_bias, value_bias, proj_bias, attn_scale, norm2_gain, norm2_shift,
            fc2_bias, mlp_scale, fc1_bias, (valid_len // 32).astype(BF), (valid_len % 32).astype(BF),
        ]
    )
    x = spread(tokens)
    small_all = lax.all_gather(small, "fsdp", axis=0).astype(F32)
    part = width // groups
    vectors = [small_all[:, i * part : (i + 1) * part].reshape(1, width) for i in range(10)]
    gain1, shift1, bias_q, bias_v, bias_p, scale1, gain2, shift2, bias_2, scale2 = vectors
    ff_part = fc1_bias.shape[0]
    bias_1 = small_all[:, 10 * part : 10 * part + ff_part].reshape(1, -1)
    rest = small_all[:, 10 * part + ff_part :].reshape(groups, 2, images_here)
    lengths = (rest[:, 0] * 32 + rest[:, 1]).astype(jnp.int32)
    column = group // 2
    length = lax.dynamic_slice(lengths, (column * 2 + place // 2, place % 2), (1, 1))[0, 0]

    def positions(which):
        base = jnp.arange(tok_here, dtype=jnp.int32)
        return jnp.concatenate([base + tok_here * (2 * which + (place + turn) % 2) for turn in turns])

    own = positions(core)
    keys_at = jnp.concatenate([own, positions(1 - core)])
    lane = jnp.arange(128, dtype=jnp.int32)[None, :]
    masked = jnp.where(keys_at < length, 0.0, -1e30)[:, None]
    mask = jnp.where(lane == 0, masked, jnp.where(lane < 4, 1.0, 0.0)).astype(BF)
    live = (own < length).astype(F32)[:, None]
    zero = jnp.zeros((1, width), F32)
    vec1 = jnp.concatenate([gain1, shift1] + [zero] * 6)
    vec2 = jnp.concatenate([bias_p, scale1, gain2, shift2, bias_2, scale2, zero, zero])
    bias_all = jnp.concatenate([bias_q, zero, bias_v], axis=1)

    wq = lax.all_gather(qkv_weight, "fsdp", axis=0, tiled=True)
    normed, q, kv = qkv(x, vec1, wq, bias_all)
    kv_other = lax.ppermute(kv, "fsdp", swap)
    cot = spread(cotangent)
    wp = lax.all_gather(proj_weight, "fsdp", axis=0, tiled=True)
    w1 = lax.all_gather(fc1_weight, "fsdp", axis=0, tiled=True)
    w2 = lax.all_gather(fc2_weight, "fsdp", axis=0, tiled=True)
    attended, stats = att_fwd(q, kv, kv_other, mask, FWD_BLOCKS(rows))
    mixed, grad_mid, grad_att, dwp, dw1, dw2, small2, grad_b1 = mlp(attended, x, cot, live, vec2, wp, w1, bias_1, w2)
    mixed_out = collect(mixed)
    scatter = lambda v: lax.psum_scatter(v, "fsdp", scatter_dimension=0, tiled=True)
    dw2_part = scatter(dw2)
    dw1_part = scatter(dw1)
    dwp_part = scatter(dwp)
    dq, dko, dkp, dvo, dvp = att_bwd(q, kv, kv_other, mask, stats, grad_att, attended, (rows, rows))
    dkr = lax.ppermute(dkp, "fsdp", swap)
    dvr = lax.ppermute(dvp, "fsdp", swap)
    dwq, grad_x, small1 = qback(dq, dko, dvo, dkr, dvr, x, normed, grad_mid, vec1, wq)
    input_grad = collect(grad_x).astype(F32)
    dwq_part = scatter(dwq)
    totals = lax.psum((dw2_part, dw1_part, dwp_part), "seq")
    total_q = lax.psum(dwq_part, "seq")
    image = jnp.arange(groups * images_here, dtype=jnp.int32)
    mine = image == (column * 2 + place // 2) * images_here + place % 2
    squares = jnp.sum(small2[8:13], axis=1)
    squares = jnp.where(mine[:, None], squares[None, :], 0.0)
    sums = jnp.concatenate(
        [
            small1[2], small1[3], small1[0], small1[1], small2[5], small2[4], small2[2], small2[3],
            small2[1], small2[0], grad_b1[0], squares.reshape(-1),
        ]
    )
    sums = lax.psum(sums, AXES)
    grads = [lax.dynamic_slice(sums, (i * width + group * part,), (part,)) for i in range(10)]
    g_gain1, g_shift1, g_bq, g_bv, g_bp, g_scale1, g_gain2, g_shift2, g_b2, g_scale2 = grads
    g_b1 = lax.dynamic_slice(sums, (10 * width + group * ff_part,), (ff_part,))
    squares = sums[10 * width + groups * ff_part :].reshape(groups * images_here, 5)
    squares = lax.dynamic_slice(squares, (group * images_here, 0), (images_here, 5))
    rms = jnp.sqrt(squares / (valid_len.astype(F32)[:, None] * width))
    return (
        mixed_out, input_grad, rms, g_gain1, g_shift1, total_q.astype(F32), g_bq, g_bv, totals[2].astype(F32), g_bp,
        g_scale1, g_gain2, g_shift2, totals[1].astype(F32), g_b1, totals[0].astype(F32), g_b2, g_scale2,
    )


def FWD_BLOCKS(rows):
    first = (rows // 2 + 15) // 16 * 16
    return (first, rows - first)


def solution(mesh):
    in_specs = (
        P("fsdp", "seq", None),
        P("fsdp"),
        P("fsdp", "seq", None),
        P("fsdp"),
        P("fsdp"),
        P("fsdp", None),
        P("fsdp"),
        P("fsdp"),
        P("fsdp", None),
        P("fsdp"),
        P("fsdp"),
        P("fsdp"),
        P("fsdp"),
        P("fsdp", None),
        P("fsdp"),
        P("fsdp", None),
        P("fsdp"),
        P("fsdp"),
    )
    out_specs = (
        P("fsdp", "seq", None),
        P("fsdp", "seq", None),
        P("fsdp", None),
        P("fsdp"),
        P("fsdp"),
        P("fsdp", None),
        P("fsdp"),
        P("fsdp"),
        P("fsdp", None),
        P("fsdp"),
        P("fsdp"),
        P("fsdp"),
        P("fsdp"),
        P("fsdp", None),
        P("fsdp"),
        P("fsdp", None),
        P("fsdp"),
        P("fsdp"),
    )
    seq_count = mesh.shape["seq"]
    paired = seq_count == 4 and mesh.shape["fsdp"] % 2 == 0
    return jax.shard_map(
        fast_device if paired else generic_device, mesh=mesh, in_specs=in_specs, out_specs=out_specs, check_vma=False
    )
```

```python
import functools

import jax
import jax.numpy as jnp
from jax import lax
from jax.experimental import pallas as pl
from jax.experimental.pallas import tpu as pltpu
from jax.sharding import PartitionSpec as P

EPSILON = 1e-06
HEAD_DIM = 64


def for_sending(value):
    return jax.tree.map(lambda a: a.astype(jnp.bfloat16) if a.dtype == jnp.float32 else a, value)


def layer_norm(values, gain, shift):
    average = jnp.mean(values, axis=-1, keepdims=True)
    centered = values - average
    variance = jnp.mean(centered * centered, axis=-1, keepdims=True)
    return centered * lax.rsqrt(variance + EPSILON) * gain + shift


def gelu_exact(values):
    return jax.nn.gelu(values, approximate=False)


def block_rows(length):
    return length // 2


def attend_image(inputs_one):
    queries, keys_in, values_in, length_one = inputs_one
    length = queries.shape[0]
    rows = block_rows(length)
    scaling = queries.shape[2] ** (-0.5)
    live_keys = (jnp.arange(length, dtype=jnp.int32) < length_one)[None, None, :]
    outputs = []
    totals = []
    for section in range(length // rows):
        part_q = queries[section * rows : (section + 1) * rows]
        scores = (
            jnp.einsum("qhe,khe->hqk", part_q, keys_in, preferred_element_type=jnp.float32)
            * scaling
        )
        scores = jnp.where(live_keys, scores, -1e30)
        highest = jnp.max(scores, axis=-1, keepdims=True)
        exponent = jnp.exp(scores - highest)
        row_sums = jnp.sum(exponent, axis=-1, keepdims=True)
        probabilities = (exponent / row_sums).astype(jnp.bfloat16)
        outputs.append(
            jnp.einsum("hqk,khe->qhe", probabilities, values_in, preferred_element_type=jnp.float32)
        )
        totals.append(highest + jnp.log(row_sums))
    return (jnp.concatenate(outputs, axis=0).astype(jnp.bfloat16), jnp.concatenate(totals, axis=1))


def attend_back(inputs_one):
    queries, keys_in, values_in, grad_out, log_total, length_one = inputs_one
    length = queries.shape[0]
    rows = block_rows(length)
    scaling = queries.shape[2] ** (-0.5)
    live_keys = (jnp.arange(length, dtype=jnp.int32) < length_one)[None, None, :]
    grad_keys = jnp.zeros(keys_in.shape, jnp.float32)
    grad_values = jnp.zeros(values_in.shape, jnp.float32)
    grad_queries = []
    for section in range(length // rows):
        part_q = queries[section * rows : (section + 1) * rows]
        part_grad = grad_out[section * rows : (section + 1) * rows]
        part_total = log_total[:, section * rows : (section + 1) * rows]
        scores = (
            jnp.einsum("qhe,khe->hqk", part_q, keys_in, preferred_element_type=jnp.float32)
            * scaling
        )
        scores = jnp.where(live_keys, scores, -1e30)
        probabilities = jnp.exp(scores - part_total)
        rounded = probabilities.astype(jnp.bfloat16)
        grad_prob = jnp.einsum(
            "qhe,khe->hqk", part_grad, values_in, preferred_element_type=jnp.float32
        )
        centre = jnp.sum(probabilities * grad_prob, axis=-1, keepdims=True)
        grad_scores = (probabilities * (grad_prob - centre)).astype(jnp.bfloat16)
        grad_queries.append(
            jnp.einsum("hqk,khe->qhe", grad_scores, keys_in, preferred_element_type=jnp.float32)
            * scaling
        )
        grad_keys = (
            grad_keys
            + jnp.einsum("hqk,qhe->khe", grad_scores, part_q, preferred_element_type=jnp.float32)
            * scaling
        )
        grad_values = grad_values + jnp.einsum(
            "hqk,qhe->khe", rounded, part_grad, preferred_element_type=jnp.float32
        )
    stacked = jnp.stack([jnp.concatenate(grad_queries, axis=0), grad_keys, grad_values], axis=1)
    return stacked.astype(jnp.bfloat16)


def generic_device(
    tokens,
    valid_len,
    cotangent,
    norm1_gain,
    norm1_shift,
    qkv_weight,
    query_bias,
    value_bias,
    proj_weight,
    proj_bias,
    attn_scale,
    norm2_gain,
    norm2_shift,
    fc1_weight,
    fc1_bias,
    fc2_weight,
    fc2_bias,
    mlp_scale,
):
    gathered = (
        lax.all_gather(norm1_gain, "fsdp", axis=0, tiled=True),
        lax.all_gather(norm1_shift, "fsdp", axis=0, tiled=True),
        lax.all_gather(qkv_weight, "fsdp", axis=0, tiled=True),
        lax.all_gather(query_bias, "fsdp", axis=0, tiled=True),
        lax.all_gather(value_bias, "fsdp", axis=0, tiled=True),
        lax.all_gather(proj_weight, "fsdp", axis=0, tiled=True),
        lax.all_gather(proj_bias, "fsdp", axis=0, tiled=True),
        lax.all_gather(attn_scale, "fsdp", axis=0, tiled=True),
        lax.all_gather(norm2_gain, "fsdp", axis=0, tiled=True),
        lax.all_gather(norm2_shift, "fsdp", axis=0, tiled=True),
        lax.all_gather(fc1_weight, "fsdp", axis=0, tiled=True),
        lax.all_gather(fc1_bias, "fsdp", axis=0, tiled=True),
        lax.all_gather(fc2_weight, "fsdp", axis=0, tiled=True),
        lax.all_gather(fc2_bias, "fsdp", axis=0, tiled=True),
        lax.all_gather(mlp_scale, "fsdp", axis=0, tiled=True),
    )
    (
        gain_one,
        shift_one,
        weight_qkv,
        bias_query,
        bias_value,
        weight_proj,
        bias_proj,
        scale_one,
        gain_two,
        shift_two,
        weight_up,
        bias_up,
        weight_down,
        bias_down,
        scale_two,
    ) = gathered
    images_here, tok_here, width = tokens.shape
    seq_count = lax.axis_size("seq")
    head_cols = width // seq_count
    heads_here = head_cols // HEAD_DIM
    length = tok_here * seq_count
    inputs_f = tokens.astype(jnp.float32)
    gain_first = gain_one.astype(jnp.float32)
    shift_first = shift_one.astype(jnp.float32)
    gain_second = gain_two.astype(jnp.float32)
    shift_second = shift_two.astype(jnp.float32)
    scale_first = scale_one.astype(jnp.float32)
    scale_second = scale_two.astype(jnp.float32)
    normed_first = layer_norm(inputs_f, gain_first, shift_first).astype(jnp.bfloat16)
    bias_all = jnp.concatenate(
        [
            bias_query.astype(jnp.float32),
            jnp.zeros((width,), jnp.float32),
            bias_value.astype(jnp.float32),
        ]
    )
    projected = (
        jnp.einsum("mtd,de->mte", normed_first, weight_qkv, preferred_element_type=jnp.float32)
        + bias_all
    ).astype(jnp.bfloat16)
    by_heads = lax.all_to_all(
        projected.reshape(images_here, tok_here, 3, seq_count, head_cols),
        "seq",
        split_axis=3,
        concat_axis=1,
        tiled=True,
    )
    by_heads = by_heads.reshape(images_here, length, 3, heads_here, HEAD_DIM)
    attended, log_total = lax.map(
        attend_image, (by_heads[:, :, 0], by_heads[:, :, 1], by_heads[:, :, 2], valid_len)
    )
    attended_tok = lax.all_to_all(
        for_sending(attended.reshape(images_here, length, 1, head_cols)),
        "seq",
        split_axis=1,
        concat_axis=2,
        tiled=True,
    )
    attended_tok = attended_tok.reshape(images_here, tok_here, width)
    attn_out = jnp.einsum(
        "mtd,de->mte", attended_tok, weight_proj, preferred_element_type=jnp.float32
    ) + bias_proj.astype(jnp.float32)
    branch_attn = scale_first * attn_out
    middle = inputs_f + branch_attn
    normed_second = layer_norm(middle, gain_second, shift_second).astype(jnp.bfloat16)
    hidden_pre = jnp.einsum(
        "mtd,df->mtf", normed_second, weight_up, preferred_element_type=jnp.float32
    ) + bias_up.astype(jnp.float32)
    hidden = gelu_exact(hidden_pre).astype(jnp.bfloat16)
    mlp_out = jnp.einsum(
        "mtf,fd->mtd", hidden, weight_down, preferred_element_type=jnp.float32
    ) + bias_down.astype(jnp.float32)
    branch_mlp = scale_second * mlp_out
    result = middle + branch_mlp
    positions = lax.axis_index("seq") * tok_here + jnp.arange(tok_here, dtype=jnp.int32)
    live = (positions[None, :] < valid_len[:, None]).astype(jnp.float32)[:, :, None]
    squares = jnp.stack(
        [
            jnp.sum(live * piece * piece, axis=(1, 2))
            for piece in (inputs_f, branch_attn, middle, branch_mlp, result)
        ],
        axis=-1,
    )
    squares = lax.psum(squares, "seq")
    rms_stats = jnp.sqrt(squares / (valid_len.astype(jnp.float32)[:, None] * width))
    grad_result = cotangent.astype(jnp.float32)
    grad_mlp_scale = jnp.sum(grad_result * mlp_out, axis=(0, 1))
    grad_mlp_out = (grad_result * scale_second).astype(jnp.bfloat16)
    grad_fc2_bias = jnp.sum(grad_mlp_out, axis=(0, 1), dtype=jnp.float32)
    grad_fc2_weight = jnp.einsum(
        "mtf,mtd->fd", hidden, grad_mlp_out, preferred_element_type=jnp.float32
    )
    grad_hidden = jnp.einsum(
        "mtd,fd->mtf", grad_mlp_out, weight_down, preferred_element_type=jnp.float32
    )
    gelu_value, gelu_back = jax.vjp(gelu_exact, hidden_pre)
    grad_pre = gelu_back(grad_hidden)[0].astype(jnp.bfloat16)
    grad_fc1_bias = jnp.sum(grad_pre, axis=(0, 1), dtype=jnp.float32)
    grad_fc1_weight = jnp.einsum(
        "mtd,mtf->df", normed_second, grad_pre, preferred_element_type=jnp.float32
    )
    grad_normed_second = jnp.einsum(
        "mtf,df->mtd", grad_pre, weight_up, preferred_element_type=jnp.float32
    )
    norm_value, norm_back = jax.vjp(layer_norm, middle, gain_second, shift_second)
    grad_middle_norm, grad_norm2_gain, grad_norm2_shift = norm_back(grad_normed_second)
    grad_middle = grad_result + grad_middle_norm
    grad_attn_scale = jnp.sum(grad_middle * attn_out, axis=(0, 1))
    grad_attn_out = (grad_middle * scale_first).astype(jnp.bfloat16)
    grad_proj_bias = jnp.sum(grad_attn_out, axis=(0, 1), dtype=jnp.float32)
    grad_proj_weight = jnp.einsum(
        "mtd,mte->de", attended_tok, grad_attn_out, preferred_element_type=jnp.float32
    )
    grad_attended = jnp.einsum(
        "mte,de->mtd", grad_attn_out, weight_proj, preferred_element_type=jnp.float32
    ).astype(jnp.bfloat16)
    grad_heads = lax.all_to_all(
        grad_attended.reshape(images_here, tok_here, seq_count, head_cols),
        "seq",
        split_axis=2,
        concat_axis=1,
        tiled=True,
    )
    grad_heads = grad_heads.reshape(images_here, length, heads_here, HEAD_DIM)
    grad_qkv = lax.map(
        attend_back,
        (by_heads[:, :, 0], by_heads[:, :, 1], by_heads[:, :, 2], grad_heads, log_total, valid_len),
    )
    grad_projected = lax.all_to_all(
        for_sending(grad_qkv.reshape(images_here, length, 3, 1, head_cols)),
        "seq",
        split_axis=1,
        concat_axis=3,
        tiled=True,
    )
    grad_projected = grad_projected.reshape(images_here, tok_here, 3 * width)
    grad_query_bias = jnp.sum(grad_projected[:, :, :width], axis=(0, 1), dtype=jnp.float32)
    grad_value_bias = jnp.sum(grad_projected[:, :, 2 * width :], axis=(0, 1), dtype=jnp.float32)
    grad_qkv_weight = jnp.einsum(
        "mtd,mte->de", normed_first, grad_projected, preferred_element_type=jnp.float32
    )
    grad_normed_first = jnp.einsum(
        "mte,de->mtd", grad_projected, weight_qkv, preferred_element_type=jnp.float32
    )
    first_value, first_back = jax.vjp(layer_norm, inputs_f, gain_first, shift_first)
    grad_input_norm, grad_norm1_gain, grad_norm1_shift = first_back(grad_normed_first)
    input_grad = grad_middle + grad_input_norm
    reduced = (
        lax.psum_scatter(grad_norm1_gain, "fsdp", scatter_dimension=0, tiled=True),
        lax.psum_scatter(grad_norm1_shift, "fsdp", scatter_dimension=0, tiled=True),
        lax.psum_scatter(grad_qkv_weight, "fsdp", scatter_dimension=0, tiled=True),
        lax.psum_scatter(grad_query_bias, "fsdp", scatter_dimension=0, tiled=True),
        lax.psum_scatter(grad_value_bias, "fsdp", scatter_dimension=0, tiled=True),
        lax.psum_scatter(grad_proj_weight, "fsdp", scatter_dimension=0, tiled=True),
        lax.psum_scatter(grad_proj_bias, "fsdp", scatter_dimension=0, tiled=True),
        lax.psum_scatter(grad_attn_scale, "fsdp", scatter_dimension=0, tiled=True),
        lax.psum_scatter(grad_norm2_gain, "fsdp", scatter_dimension=0, tiled=True),
        lax.psum_scatter(grad_norm2_shift, "fsdp", scatter_dimension=0, tiled=True),
        lax.psum_scatter(grad_fc1_weight, "fsdp", scatter_dimension=0, tiled=True),
        lax.psum_scatter(grad_fc1_bias, "fsdp", scatter_dimension=0, tiled=True),
        lax.psum_scatter(grad_fc2_weight, "fsdp", scatter_dimension=0, tiled=True),
        lax.psum_scatter(grad_fc2_bias, "fsdp", scatter_dimension=0, tiled=True),
        lax.psum_scatter(grad_mlp_scale, "fsdp", scatter_dimension=0, tiled=True),
    )
    reduced = lax.psum(
        (
            reduced[0],
            reduced[1],
            reduced[2],
            reduced[3],
            reduced[4],
            reduced[5],
            reduced[6],
            reduced[7],
            reduced[8],
            reduced[9],
            reduced[10],
            reduced[11],
            reduced[12],
            reduced[13],
            reduced[14],
        ),
        "seq",
    )
    return (
        result.astype(jnp.bfloat16),
        input_grad,
        rms_stats,
        reduced[0],
        reduced[1],
        reduced[2],
        reduced[3],
        reduced[4],
        reduced[5],
        reduced[6],
        reduced[7],
        reduced[8],
        reduced[9],
        reduced[10],
        reduced[11],
        reduced[12],
        reduced[13],
        reduced[14],
    )


NT = (((1,), (1,)), ((), ()))
NN = (((1,), (0,)), ((), ()))
TN = (((0,), (0,)), ((), ()))

def dotf(a, b, dims):
    return lax.dot_general(a, b, dims, preferred_element_type=jnp.float32)

def att_fwd_kernel(blocks, q_ref, ko_ref, kp_ref, vo_ref, vp_ref, bias_ref, o_ref, st_ref, kbuf, vbuf):
    rows = q_ref.shape[0]
    kbuf[:rows, :128] = ko_ref[...]
    kbuf[rows:, :128] = kp_ref[...]
    vbuf[:rows, :128] = vo_ref[...]
    vbuf[rows:, :128] = vp_ref[...]

    @pl.when(pl.program_id(0) == 0)
    def _():
        kbuf[:, 128:] = bias_ref[...]
        vbuf[:, 128:] = jnp.ones_like(vbuf[:, 128:])

    start = 0
    for size in blocks:
        lane = lax.broadcasted_iota(jnp.int32, (size, 128), 1)
        low = lane < 64
        first = (lane == 0).astype(jnp.bfloat16)
        q = q_ref[start:start + size, :]
        heads = []
        for h in range(2):
            keep = low if h == 0 else jnp.logical_not(low)
            qm = jnp.where(keep, q, jnp.zeros_like(q))
            qx = jnp.concatenate([qm, first], axis=1)
            s = dotf(qx, kbuf[...], NT)
            m = jnp.max(s, axis=-1, keepdims=True)
            p = jnp.exp(s - m).astype(jnp.bfloat16)
            ol = dotf(p, vbuf[...], NN)
            l = ol[:, 128:]
            heads.append(ol[:, :128] / l)
            total = -(m + jnp.log(l))
            hi = total.astype(jnp.bfloat16).astype(jnp.float32)
            mid = (total - hi).astype(jnp.bfloat16).astype(jnp.float32)
            lo = total - hi - mid
            piece = jnp.where(lane == 0, 1.0, jnp.where(lane == 1, hi, jnp.where(lane == 2, mid, jnp.where(lane == 3, lo, 0.0))))
            st_ref[h, start:start + size, :] = piece.astype(jnp.bfloat16)
        o_ref[start:start + size, :] = jnp.where(low, heads[0], heads[1]).astype(jnp.bfloat16)
        start += size

def att_fwd(q, kv_own, kv_other, bias, blocks):
    rows, width = q.shape
    pairs = width // 128
    heads = width // 64
    return pl.pallas_call(
        functools.partial(att_fwd_kernel, blocks),
        grid=(pairs,),
        in_specs=[
            pl.BlockSpec((rows, 128), lambda i: (0, i)),
            pl.BlockSpec((rows, 128), lambda i: (0, i)),
            pl.BlockSpec((rows, 128), lambda i: (0, i)),
            pl.BlockSpec((rows, 128), lambda i: (0, i + pairs)),
            pl.BlockSpec((rows, 128), lambda i: (0, i + pairs)),
            pl.BlockSpec((2 * rows, 128), lambda i: (0, 0)),
        ],
        out_specs=[
            pl.BlockSpec((rows, 128), lambda i: (0, i)),
            pl.BlockSpec((2, rows, 128), lambda i: (i, 0, 0)),
        ],
        out_shape=[
            jax.ShapeDtypeStruct((rows, width), jnp.bfloat16),
            jax.ShapeDtypeStruct((heads, rows, 128), jnp.bfloat16),
        ],
        scratch_shapes=[pltpu.VMEM((2 * rows, 256), jnp.bfloat16), pltpu.VMEM((2 * rows, 256), jnp.bfloat16)],
        compiler_params=pltpu.CompilerParams(vmem_limit_bytes=56 * 2**20),
        name="att_fwd",
    )(q, kv_own, kv_other, kv_own, kv_other, bias)

F32 = jnp.float32
BF = jnp.bfloat16

def norm_parts(v):
    mean = jnp.mean(v, axis=-1, keepdims=True)
    cen = v - mean
    var = jnp.mean(cen * cen, axis=-1, keepdims=True)
    r = lax.rsqrt(var + EPSILON)
    return cen * r, r

def norm_back(z, r, grad, gain):
    e = grad * gain
    return r * (e - jnp.mean(e, axis=-1, keepdims=True) - z * jnp.mean(e * z, axis=-1, keepdims=True))

def mlp_kernel(att_ref, x_ref, cot_ref, live_ref, vec_ref, wp_ref, w1_ref, b1_ref, w2_ref,
               mixed_ref, gmid_ref, gatt_ref, dwp_ref, dw1_ref, dw2_ref, small_ref,
               ao, n2, n2t, gm, acc, gn2):
    step = pl.program_id(0)
    part = att_ref.shape[1] // small_ref.shape[0]
    half = att_ref.shape[0] // 2
    last = pl.num_programs(0) - 1

    @pl.when(step == 0)
    def _():
        a = dotf(att_ref[...], wp_ref[...], NN) + vec_ref[0:1, :]
        ao[...] = a
        mid = x_ref[...].astype(F32) + vec_ref[1:2, :] * a
        gmid_ref[...] = mid
        z, _r = norm_parts(mid)
        n = (z * vec_ref[2:3, :] + vec_ref[3:4, :]).astype(BF)
        n2[...] = n
        n2t[...] = n.T
        gm[...] = (cot_ref[...].astype(F32) * vec_ref[5:6, :]).astype(BF)
        acc[...] = jnp.broadcast_to(vec_ref[4:5, :], acc.shape)
        gn2[...] = jnp.zeros_like(gn2)

    u = dotf(n2[...], w1_ref[...], NN) + b1_ref[...]
    phi = 0.5 + 0.5 * lax.erf(u * 0.7071067811865476)
    hid = (u * phi).astype(BF)
    slope = phi + u * jnp.exp(u * u * -0.5) * 0.3989422804014327
    gh = dotf(gm[...], w2_ref[...], NT)
    gpf = gh * slope
    gp = gpf.astype(BF)
    gb1 = jnp.sum(gp.astype(F32), axis=0, keepdims=True)
    for i in range(gb1.shape[1] // part):
        small_ref[step, 10 + i:11 + i, :] = gb1[:, i * part:(i + 1) * part]
    acc[...] += dotf(hid, w2_ref[...], NN)
    gn2[...] += dotf(gp, w1_ref[...], NT)
    dw2_ref[...] = dotf(hid, gm[...], TN).astype(BF)
    dw1_ref[...] = dotf(n2t[...], gp, NN).astype(BF)

    @pl.when(step == last)
    def _():
        out = acc[...]
        cot = cot_ref[...].astype(F32)
        live = live_ref[...]
        x = x_ref[...].astype(F32)
        mid = gmid_ref[...]
        branch = vec_ref[5:6, :] * out
        res = mid + branch
        low = res.astype(BF)
        mixed_ref[0, :half] = low[:half]
        mixed_ref[1, :half] = low[half:]
        mixed_ref[:, half:] = jnp.zeros_like(mixed_ref[:, half:])
        groups = small_ref.shape[0]

        def put(row, v):
            for i in range(groups):
                small_ref[i, row:row + 1, :] = v[:, i * part:(i + 1) * part]

        col = lambda v: jnp.sum(v, axis=0, keepdims=True)
        put(0, col(cot * out))
        put(1, col(gm[...].astype(F32)))
        ba = vec_ref[1:2, :] * ao[...]
        place = lax.axis_index("seq")
        owner = lax.axis_index("fsdp") // 2 * 2 + place // 2
        lane = lax.broadcasted_iota(jnp.int32, (1, part), 1)
        line = jnp.zeros((1, part), F32)
        for i, v in enumerate((x, ba, mid, branch, res)):
            line = jnp.where(lane == place % 2 * 5 + i, jnp.sum(col(live * v * v), axis=1, keepdims=True), line)
        for i in range(groups):
            small_ref[i, 14:15, :] = jnp.where(owner == i, line, 0.0)
            small_ref[i, 15:16, :] = jnp.zeros_like(line)
        z, r = norm_parts(mid)
        g = gn2[...]
        put(2, col(g * z))
        put(3, col(g))
        gmid = cot + norm_back(z, r, g, vec_ref[2:3, :])
        gmid_ref[...] = gmid
        put(4, col(gmid * ao[...]))
        gao = (gmid * vec_ref[1:2, :]).astype(BF)
        put(5, col(gao.astype(F32)))
        gatt_ref[...] = dotf(gao, wp_ref[...], NT).astype(BF)
        dwp_ref[...] = dotf(att_ref[...], gao, TN).astype(BF)

def mlp(att, x, cot, live, vec, wp, w1, b1, w2, groups):
    rows, width = att.shape
    ff = w1.shape[1]
    fc = ff // groups
    pad = (rows // 2 + 15) // 16 * 16
    full = lambda s: pl.BlockSpec(s, lambda j: (0,) * len(s))
    sd = jax.ShapeDtypeStruct
    return pl.pallas_call(
        mlp_kernel, grid=(ff // fc,),
        in_specs=[full((rows, width)), full((rows, width)), full((rows, width)), full((rows, 1)), full((8, width)), full((width, width)),
            pl.BlockSpec((width, fc), lambda j: (0, j)), pl.BlockSpec((1, fc), lambda j: (0, j)), pl.BlockSpec((fc, width), lambda j: (j, 0))],
        out_specs=[full((2, pad, width)), full((rows, width)), full((rows, width)), full((width, width)),
            pl.BlockSpec((width, fc), lambda j: (0, j)), pl.BlockSpec((fc, width), lambda j: (j, 0)), full((groups, 16, width // groups))],
        out_shape=[sd((2, pad, width), BF), sd((rows, width), F32), sd((rows, width), BF), sd((width, width), BF), sd((width, ff), BF), sd((ff, width), BF), sd((groups, 16, width // groups), F32)],
        scratch_shapes=[pltpu.VMEM((rows, width), F32), pltpu.VMEM((rows, width), BF), pltpu.VMEM((width, rows), BF), pltpu.VMEM((rows, width), BF), pltpu.VMEM((rows, width), F32), pltpu.VMEM((rows, width), F32)],
        compiler_params=pltpu.CompilerParams(vmem_limit_bytes=60 * 2**20), name="mlp",
    )(att, x, cot, live, vec, wp, w1, b1, w2)

def qkv_kernel(x_ref, vec_ref, w_ref, b_ref, nt_ref, q_ref, kv_ref, n1):
    step = pl.program_id(0)
    @pl.when(step == 0)
    def _():
        z, _r = norm_parts(x_ref[...].astype(F32))
        n = (z * vec_ref[0:1, :] + vec_ref[1:2, :]).astype(BF)
        n1[...] = n
        nt_ref[...] = n.T
    w = w_ref.shape[1]
    y = (dotf(n1[...], w_ref[...], NN) + b_ref[...]).astype(BF)
    @pl.when(step == 2)
    def _():
        q_ref[...] = y * jnp.asarray(0.125, BF)
    @pl.when(step != 2)
    def _():
        kv_ref[...] = y

def qkv(x, vec, w, b):
    rows, width = x.shape
    full = lambda s: pl.BlockSpec(s, lambda j: (0,) * len(s))
    sd = jax.ShapeDtypeStruct
    rot = lambda j: (0, (j + 1) % 3)
    return pl.pallas_call(qkv_kernel, grid=(3,),
        in_specs=[full((rows, width)), full((8, width)), pl.BlockSpec((width, width), rot), pl.BlockSpec((1, width), rot)],
        out_specs=[full((width, rows)), full((rows, width)), pl.BlockSpec((rows, width), lambda j: (0, jnp.minimum(j, 1)))],
        out_shape=[sd((width, rows), BF), sd((rows, width), BF), sd((rows, 2 * width), BF)],
        scratch_shapes=[pltpu.VMEM((rows, width), BF)],
        compiler_params=pltpu.CompilerParams(vmem_limit_bytes=56 * 2**20), name="qkv")(x, vec, w, b)


MESH = pl.DeviceIdType.MESH


def places():
    f = lax.axis_index("fsdp")
    z = lax.axis_index("seq")
    core = f % 2
    dx = 2 - 4 * (f // 2 % 2)
    dy = 4 - 8 * (f // 4)
    da = (1 - core) * dx + core * dy
    db = core * dx + (1 - core) * dy
    mate = f + 1 - 2 * core
    return f, z, mate, da, db


def reduce_scratch(rows, cols, chunks, kind, copied=True):
    dma = pltpu.SemaphoreType.DMA
    bufs = [pltpu.VMEM((n, rows, cols), kind) for n in (4, 3, 2)] + [pltpu.VMEM((rows, cols), kind)]
    sems = [dma((chunks, n)) for n in (4, 4, 3, 3, 2, 2)]
    if copied:
        bufs.append(pltpu.VMEM((4, rows, cols), kind))
        sems.append(dma((chunks, 4)))
    return bufs + sems


REDUCE_REFS = 10
REDUCE_REFS_COPIED = 12


def reduce_steps(src, out, scratch, cuts, copied=True):
    if copied:
        yours, came, zin, tot, mine, ex_send, ex_recv, l_send, l_recv, z_send, z_recv, load_sem = scratch
    else:
        yours, came, zin, tot, ex_send, ex_recv, l_send, l_recv, z_send, z_recv = scratch
    f, z, mate, da, db = places()
    own = (f + da + db, f + db, f + da, f)
    other = (mate + da + db, mate + da, mate + db, mate)
    outer = z % 3 == 0
    inner = z % 3 != 0

    def remote(a, b, s, r, dev):
        return pltpu.make_async_remote_copy(src_ref=a, dst_ref=b, send_sem=s, recv_sem=r, device_id=dev, device_id_type=MESH)

    def steps(k, lo, size):
        at = pl.ds(lo, size)

        def held(m):
            return mine.at[m, at] if copied else src.at[own[m], at]

        def load(m):
            return pltpu.make_async_copy(src.at[own[m], at], mine.at[m, at], load_sem.at[k, m])

        def swap(m):
            return remote(src.at[other[m], at], yours.at[m, at], ex_send.at[k, m], ex_recv.at[k, m], (mate, z))

        def hop(i):
            return remote(held(i), came.at[i, at], l_send.at[k, i], l_recv.at[k, i], (f + (da if i == 2 else db), z))

        def to_inner():
            return remote(tot.at[at], zin.at[0, at], z_send.at[k, 0], z_recv.at[k, 0], (f, 1 + z // 3))

        def across():
            return remote(tot.at[at], zin.at[1, at], z_send.at[k, 0], z_recv.at[k, 1], (f, 3 - z))

        def to_outer():
            return remote(out.at[at], zin.at[1, at], z_send.at[k, 1], z_recv.at[k, 1], (f, 3 * (z - 1)))

        def merge(m):
            if copied:
                load(m).wait()
            swap(m).wait_recv()
            h = held(m)
            h[...] = h[...] + yours[m, at]

        def s0():
            for m in range(4):
                swap(m).start()
                if copied:
                    load(m).start()

        def s1():
            for m in range(2):
                merge(m)
                hop(m).start()

        def s2():
            merge(2)
            hop(0).wait_recv()
            h = held(2)
            h[...] = h[...] + came[0, at]
            hop(2).start()
            merge(3)

        def s3():
            hop(1).wait_recv()
            hop(2).wait_recv()
            total = held(3)[...].astype(F32) + came[1, at].astype(F32) + came[2, at].astype(F32)
            tot[at] = total.astype(tot.dtype)

            @pl.when(outer)
            def _():
                to_inner().start()

        def s4():
            @pl.when(inner)
            def _():
                to_inner().wait_recv()
                tot[at] = tot[at] + zin[0, at]
                across().start()

        def s5():
            @pl.when(inner)
            def _():
                across().wait_recv()
                out[at] = tot[at] + zin[1, at]
                to_outer().start()

        def s6():
            @pl.when(outer)
            def _():
                to_outer().wait_recv()
                out[at] = zin[1, at]
                to_inner().wait_send()

            @pl.when(inner)
            def _():
                across().wait_send()
                to_outer().wait_send()

            for m in range(4):
                swap(m).wait_send()
            for i in range(3):
                hop(i).wait_send()

        return [s0, s1, s2, s3, s4, s5, s6]

    return [steps(k, lo, size) for k, (lo, size) in enumerate(cuts)]


def drain(every, done):
    count = len(every)
    for t in range(count + 6):
        for s in range(6, 0, -1):
            k = t - s
            if 0 <= k < count and (k, s) not in done:
                every[k][s]()


def even_cuts(rows, parts):
    size = rows // parts // 16 * 16
    cuts = [(i * size, size) for i in range(parts - 1)]
    return cuts + [((parts - 1) * size, rows - (parts - 1) * size)]


def relay_partner(f, z, turn):
    return f - f % 2 + z // 2, 2 * (f % 2) + (z + turn) % 2


def greet(relay):
    f, z, mate, da, db = places()
    barrier = pltpu.get_barrier_semaphore()

    def signal(group, place):
        pl.semaphore_signal(barrier, inc=1, device_id=(group, place), device_id_type=MESH)

    for other in (mate, f + da, f + db):
        signal(other, z)

    @pl.when(z > 0)
    def _():
        signal(f, z - 1)

    @pl.when(z < 3)
    def _():
        signal(f, z + 1)

    if relay:
        signal(*relay_partner(f, z, 1))

        @pl.when(z // 2 != f % 2)
        def _():
            signal(*relay_partner(f, z, 0))

    away = z // 2 - f % 2
    count = 4 + (z + 2) // 3 - z // 3
    pl.semaphore_wait(barrier, count + 1 + away * away if relay else count)


def relay_steps(src, out, sems):
    f, z, _mate, _da, _db = places()
    here = z // 2 == f % 2

    def copy(turn):
        return pltpu.make_async_remote_copy(
            src_ref=src.at[turn], dst_ref=out.at[z % 2], send_sem=sems.at[turn], recv_sem=sems.at[2 + turn],
            device_id=relay_partner(f, z, turn), device_id_type=MESH)

    def local():
        return pltpu.make_async_copy(src.at[0], out.at[z % 2], sems.at[0])

    def start():
        copy(1).start()

        @pl.when(here)
        def _():
            local().start()

        @pl.when(jnp.logical_not(here))
        def _():
            copy(0).start()

    def wait():
        copy(1).wait()

        @pl.when(here)
        def _():
            local().wait()

        @pl.when(jnp.logical_not(here))
        def _():
            copy(0).wait()

    return start, wait


def att_bwd_kernel(cuts, slots, q_ref, ko_ref, kp_ref, vo_ref, vp_ref, bias_ref, st_ref, do_ref, o_ref, mixed_ref, s0, s1, s2,
                   dqkv_ref, got_ref, back_ref, r0, r1, r2,
                   kbuf, vbuf, qx, dox, dkv, kv_send, kv_recv, relay_sems, *scratch):
    step = pl.program_id(0)
    last = pl.num_programs(0) - 1
    rows = q_ref.shape[0]
    f, z, mate, da, db = places()
    every = []
    for i, (src, out) in enumerate(((s0, r0), (s1, r1), (s2, r2))):
        every += reduce_steps(src, out, scratch[REDUCE_REFS_COPIED * i:REDUCE_REFS_COPIED * (i + 1)], cuts[i])
    relay_start, relay_wait = relay_steps(mixed_ref, back_ref, relay_sems)

    def give(i):
        cols = pl.ds(i * 128 if isinstance(i, int) else pl.multiple_of(i * 128, 128), 128)
        return pltpu.make_async_remote_copy(
            src_ref=dkv.at[i % 2, :, pl.ds(rows, rows)], dst_ref=got_ref.at[:, :, cols],
            send_sem=kv_send.at[i % 2], recv_sem=kv_recv.at[i], device_id=(mate, z), device_id_type=MESH)

    @pl.when(step == 0)
    def _():
        greet(True)
        for c in every:
            c[0]()
        relay_start()
        kbuf[:, 128:] = bias_ref[...]
        lane = lax.broadcasted_iota(jnp.int32, (2 * rows, 128), 1)
        vbuf[:, 128:] = (lane < 3).astype(BF)

    def hook(half):
        for at, todo in slots.items():
            if at % 2 == half:
                @pl.when(step == at // 2)
                def _(todo=todo):
                    for k, s in todo:
                        every[k][s]()

    @pl.when(step >= 2)
    def _():
        give(step - 2).wait_send()

    hook(0)
    kbuf[:rows, :128] = ko_ref[...]
    kbuf[rows:, :128] = kp_ref[...]
    vbuf[:rows, :128] = vo_ref[...]
    vbuf[rows:, :128] = vp_ref[...]
    lane = lax.broadcasted_iota(jnp.int32, (rows, 128), 1)
    low = lane < 64
    q = q_ref[...]
    do = do_ref[...]
    prod = do.astype(F32) * o_ref[...].astype(F32)
    for h in range(2):
        keep = low if h == 0 else jnp.logical_not(low)
        qx[h, :, :128] = jnp.where(keep, q, jnp.zeros_like(q))
        qx[h, :, 128:] = st_ref[h]
        dox[h, :, :128] = jnp.where(keep, do, jnp.zeros_like(do))
        total = -jnp.sum(jnp.where(keep, prod, 0.0), axis=-1, keepdims=True)
        hi = total.astype(BF).astype(F32)
        mid = (total - hi).astype(BF).astype(F32)
        lo = total - hi - mid
        piece = jnp.where(lane == 0, hi, jnp.where(lane == 1, mid, jnp.where(lane == 2, lo, 0.0)))
        dox[h, :, 128:] = piece.astype(BF)
    dqs = [None, None]
    for part in range(2):
        if part == 1:
            hook(1)
        start = part * rows
        dk = None
        dv = None
        kb = kbuf[start:start + rows, :]
        vb = vbuf[start:start + rows, :]
        for h in range(2):
            s = dotf(kb, qx[h], NT)
            dp = dotf(vb, dox[h], NT)
            p = jnp.exp(s)
            ds = (p * dp).astype(BF)
            p_low = p.astype(BF)
            dv_h = dotf(p_low, dox[h, :, :128], NN)
            dk_h = dotf(ds, qx[h, :, :128], NN)
            dv = dv_h if dv is None else dv + dv_h
            dk = dk_h if dk is None else dk + dk_h
            dq_h = dotf(kb[:, :128], ds, TN)
            dqs[h] = dq_h if dqs[h] is None else dqs[h] + dq_h
        dkv[step % 2, 0, start:start + rows, :] = dk.astype(BF)
        dkv[step % 2, 1, start:start + rows, :] = dv.astype(BF)
    dqs = [d.T for d in dqs]
    dqkv_ref[0] = (jnp.where(low, dqs[0], dqs[1]) * 0.125).astype(BF)
    dqkv_ref[1] = dkv[step % 2, 0, :rows, :]
    dqkv_ref[2] = dkv[step % 2, 1, :rows, :]
    give(step).start()

    @pl.when(step == last)
    def _():
        drain(every, {(k, s) for todo in slots.values() for k, s in todo})
        give(step - 1).wait_send()
        give(step).wait_send()
        for i in range(kv_recv.shape[0]):
            give(i).wait_recv()
        relay_wait()


def att_bwd(q, kv_own, kv_other, bias, st, do, o, mixed, sums):
    rows, width = q.shape
    pairs = width // 128
    blk = pl.BlockSpec((rows, 128), lambda i: (0, i))
    blk2 = pl.BlockSpec((rows, 128), lambda i: (0, i + pairs))
    hbm = pl.BlockSpec(memory_space=pltpu.HBM)
    parts = (4, 1, 1)
    cuts = [even_cuts(v.shape[1], p) for v, p in zip(sums, parts)]
    scratch = []
    for v, p in zip(sums, parts):
        scratch += reduce_scratch(v.shape[1], v.shape[2], p, v.dtype)
    whole = lambda v: pl.BlockSpec(v.shape[1:], lambda i: (0,) * (v.ndim - 1))
    return pl.pallas_call(
        functools.partial(att_bwd_kernel, cuts, BWD_SLOTS),
        grid=(pairs,),
        in_specs=[blk, blk, blk, blk2, blk2,
            pl.BlockSpec((2 * rows, 128), lambda i: (0, 0)),
            pl.BlockSpec((2, rows, 128), lambda i: (i, 0, 0)), blk, blk, hbm, hbm, hbm, hbm],
        out_specs=[pl.BlockSpec((3, rows, 128), lambda i: (0, 0, i)), hbm, hbm] + [whole(v) for v in sums],
        out_shape=[jax.ShapeDtypeStruct((3, rows, width), BF), jax.ShapeDtypeStruct((2, rows, width), BF), jax.ShapeDtypeStruct(mixed.shape, BF)]
        + [jax.ShapeDtypeStruct(v.shape[1:], v.dtype) for v in sums],
        scratch_shapes=[pltpu.VMEM((2 * rows, 256), BF), pltpu.VMEM((2 * rows, 256), BF),
            pltpu.VMEM((2, rows, 256), BF), pltpu.VMEM((2, rows, 256), BF), pltpu.VMEM((2, 2, 2 * rows, 128), BF),
            pltpu.SemaphoreType.DMA((2,)), pltpu.SemaphoreType.DMA((pairs,)), pltpu.SemaphoreType.DMA((4,))] + scratch,
        compiler_params=pltpu.CompilerParams(vmem_limit_bytes=62 * 2**20, collective_id=1, has_side_effects=True),
        name="att_bwd",
    )(q, kv_own, kv_other, kv_own, kv_other, bias, st, do, o, mixed, *sums)


BWD_SLOTS = {
    1: [(0, 1)],
    2: [(1, 1)],
    3: [(0, 2)],
    4: [(2, 1)],
    5: [(1, 2), (0, 3)],
    6: [(3, 1)],
    7: [(0, 4), (2, 2)],
    8: [(1, 3), (4, 1), (5, 1)],
    9: [(0, 5), (1, 4)],
    10: [(3, 2), (2, 3)],
    11: [(1, 5), (0, 6)],
    12: [(2, 4), (4, 2), (5, 2)],
    13: [(3, 3)],
    14: [(1, 6), (2, 5), (4, 3), (5, 3)],
    15: [(3, 4)],
}


def qback_kernel(cuts, half, dy_ref, got_ref, x_ref, nt_ref, gmid_ref, vec_ref, w_ref, s0,
                 back_ref, r0, rq, rs,
                 gn, dw, gx, small, relay_sems, *scratch):
    step = pl.program_id(0)
    groups, part = dw.shape[1:3]
    every = list(reduce_steps(s0, r0, scratch[:REDUCE_REFS_COPIED], cuts[0]))
    for i in range(4):
        at = REDUCE_REFS_COPIED + REDUCE_REFS * i
        refs = scratch[at:at + REDUCE_REFS]
        if i < 3:
            every += reduce_steps(dw.at[i], rq.at[i], refs, [(0, part)], False)
        else:
            every += reduce_steps(small, rs, refs, [(0, small.shape[1])], False)
    fixed = len(cuts[0])
    relay_start, relay_wait = relay_steps(gx, back_ref, relay_sems)

    def put(row, v):
        for i in range(groups):
            small[i, row:row + 1, :] = v[:, i * part:(i + 1) * part]

    col = lambda v: jnp.sum(v, axis=0, keepdims=True)

    @pl.when(step == 0)
    def _():
        greet(True)
        for c in every[:fixed]:
            c[0]()
        gn[...] = jnp.zeros_like(gn)
        small[...] = jnp.zeros_like(small)

    def do(i, y):
        dw[i] = dotf(nt_ref[...], y, NN).astype(BF).reshape(dw.shape[1:])
        every[fixed + i][0]()
        gn[...] += dotf(y, w_ref[...], NT)

    @pl.when(step == 0)
    def _():
        y = dy_ref[0]
        put(0, col(y.astype(F32)))
        do(0, y)
        for k, s in QBACK_SLOTS[0]:
            every[k][s]()

    @pl.when(step == 1)
    def _():
        do(1, (dy_ref[0].astype(F32) + got_ref[0].astype(F32)).astype(BF))
        for k, s in QBACK_SLOTS[1]:
            every[k][s]()

    @pl.when(step == 2)
    def _():
        y = (dy_ref[0].astype(F32) + got_ref[0].astype(F32)).astype(BF)
        put(1, col(y.astype(F32)))
        do(2, y)
        z, r = norm_parts(x_ref[...].astype(F32))
        g = gn[...]
        put(2, col(g * z))
        put(3, col(g))
        every[fixed + 3][0]()
        res = (gmid_ref[...] + norm_back(z, r, g, vec_ref[0:1, :])).astype(BF)
        gx[0, :half] = res[:half]
        gx[1, :half] = res[half:]
        gx[:, half:] = jnp.zeros_like(gx[:, half:])
        relay_start()
        drain(every, set(QBACK_SLOTS[0] + QBACK_SLOTS[1]))
        relay_wait()


QBACK_SLOTS = ([(0, 1), (1, 1)], [(0, 2), (2, 1), (1, 2), (0, 3)])


def qback(dy, got, x, nt, gmid, vec, w, dw1):
    rows, width = x.shape
    groups = dw1.shape[0]
    part = width // groups
    once = pl.Buffered(1)
    full = lambda s: pl.BlockSpec(s, lambda j: (0,) * len(s))
    keep = lambda s: pl.BlockSpec(s, lambda j: (0,) * len(s), pipeline_mode=once)
    hbm = pl.BlockSpec(memory_space=pltpu.HBM)
    sd = jax.ShapeDtypeStruct
    cuts = [even_cuts(dw1.shape[1], 4)]
    scratch = reduce_scratch(dw1.shape[1], dw1.shape[2], 4, BF)
    for _ in range(3):
        scratch += reduce_scratch(part, width, 1, BF, False)
    scratch += reduce_scratch(8, part, 1, F32, False)
    pad = (rows // 2 + 15) // 16 * 16
    return pl.pallas_call(functools.partial(qback_kernel, cuts, rows // 2), grid=(3,),
        in_specs=[pl.BlockSpec((1, rows, width), lambda j: (j, 0, 0)), pl.BlockSpec((1, rows, width), lambda j: (jnp.maximum(j - 1, 0), 0, 0)),
            keep((rows, width)), keep((width, rows)), keep((rows, width)), full((8, width)), pl.BlockSpec((width, width), lambda j: (0, j)), hbm],
        out_specs=[hbm, full(dw1.shape[1:]), full((3, part, width)), full((8, part))],
        out_shape=[sd((2, pad, width), BF), sd(dw1.shape[1:], BF), sd((3, part, width), BF), sd((8, part), F32)],
        scratch_shapes=[pltpu.VMEM((rows, width), F32), pltpu.VMEM((3, groups, part, width), BF),
            pltpu.VMEM((2, pad, width), BF), pltpu.VMEM((groups, 8, part), F32), pltpu.SemaphoreType.DMA((4,))] + scratch,
        compiler_params=pltpu.CompilerParams(vmem_limit_bytes=63 * 2**20, collective_id=2, has_side_effects=True), name="qback")(
            dy, got, x, nt, gmid, vec, w, dw1)


def relayout_pairs(groups, seq_count, turn):
    half = seq_count // 2
    pairs = []
    for f in range(groups):
        for z in range(seq_count):
            image = (z + turn) % half
            target = (f // 2 * 2 + z // half, f % 2 * half + image)
            pairs.append((f * seq_count + z, target[0] * seq_count + target[1]))
    return pairs


AXES = ("fsdp", "seq")


def fast_device(
    tokens,
    valid_len,
    cotangent,
    norm1_gain,
    norm1_shift,
    qkv_weight,
    query_bias,
    value_bias,
    proj_weight,
    proj_bias,
    attn_scale,
    norm2_gain,
    norm2_shift,
    fc1_weight,
    fc1_bias,
    fc2_weight,
    fc2_bias,
    mlp_scale,
):
    groups = lax.axis_size("fsdp")
    seq_count = lax.axis_size("seq")
    images_here, tok_here, width = tokens.shape
    rows = 2 * tok_here
    place = lax.axis_index("seq")
    group = lax.axis_index("fsdp")
    core = group % 2
    turns = range(2)
    pairs = [relayout_pairs(groups, seq_count, turn) for turn in turns]
    swap = [(f, f ^ 1) for f in range(groups)]

    def spread(block):
        parts = []
        for turn in turns:
            sent = lax.dynamic_index_in_dim(block, (place + turn) % 2, 0, keepdims=False)
            parts.append(lax.ppermute(sent, AXES, pairs[turn]))
        return jnp.concatenate(parts, axis=0)

    small = jnp.concatenate(
        [
            norm1_gain, norm1_shift, query_bias, value_bias, proj_bias, attn_scale, norm2_gain, norm2_shift,
            fc2_bias, mlp_scale, fc1_bias, (valid_len // 32).astype(BF), (valid_len % 32).astype(BF),
        ]
    )
    x = spread(tokens)
    small_all = lax.all_gather(small, "fsdp", axis=0).astype(F32)
    part = width // groups
    vectors = [small_all[:, i * part : (i + 1) * part].reshape(1, width) for i in range(10)]
    gain1, shift1, bias_q, bias_v, bias_p, scale1, gain2, shift2, bias_2, scale2 = vectors
    ff_part = fc1_bias.shape[0]
    bias_1 = small_all[:, 10 * part : 10 * part + ff_part].reshape(1, -1)
    rest = small_all[:, 10 * part + ff_part :].reshape(groups, 2, images_here)
    lengths = (rest[:, 0] * 32 + rest[:, 1]).astype(jnp.int32)
    column = group // 2
    length = lax.dynamic_slice(lengths, (column * 2 + place // 2, place % 2), (1, 1))[0, 0]

    def positions(which):
        base = jnp.arange(tok_here, dtype=jnp.int32)
        return jnp.concatenate([base + tok_here * (2 * which + (place + turn) % 2) for turn in turns])

    own = positions(core)
    keys_at = jnp.concatenate([own, positions(1 - core)])
    lane = jnp.arange(128, dtype=jnp.int32)[None, :]
    masked = jnp.where(keys_at < length, 0.0, -1e30)[:, None]
    mask = jnp.where(lane == 0, masked, jnp.where(lane < 4, 1.0, 0.0)).astype(BF)
    live = (own < length).astype(F32)[:, None]
    zero = jnp.zeros((1, width), F32)
    vec1 = jnp.concatenate([gain1, shift1] + [zero] * 6)
    vec2 = jnp.concatenate([bias_p, scale1, gain2, shift2, bias_2, scale2, zero, zero])
    bias_all = jnp.concatenate([bias_q, zero, bias_v], axis=1)

    wq = lax.all_gather(qkv_weight, "fsdp", axis=0, tiled=True)
    normed_t, q, kv = qkv(x, vec1, wq, bias_all)
    kv_other = lax.ppermute(kv, "fsdp", swap)
    cot = spread(cotangent)
    wp = lax.all_gather(proj_weight, "fsdp", axis=0, tiled=True)
    w1 = lax.all_gather(fc1_weight, "fsdp", axis=0, tiled=True)
    w2 = lax.all_gather(fc2_weight, "fsdp", axis=0, tiled=True)
    attended, stats = att_fwd(q, kv, kv_other, mask, FWD_BLOCKS(rows))
    mixed, grad_mid, grad_att, dwp, dw1, dw2, small2 = mlp(attended, x, cot, live, vec2, wp, w1, bias_1, w2, groups)
    cut = lambda v: v.reshape(groups, v.shape[0] // groups, v.shape[1])
    dqkv, got, mixed_out, total_2, total_p, sums2 = att_bwd(
        q, kv, kv_other, mask, stats, grad_att, attended, mixed, (cut(dw2), cut(dwp), small2)
    )
    grad_x, total_1, total_q, sums1 = qback(dqkv, got, x, normed_t, grad_mid, vec1, wq, cut(dw1))
    total_q = jnp.concatenate([total_q[0], total_q[1], total_q[2]], axis=1).astype(F32)
    squares = sums2[14, : images_here * 5].reshape(images_here, 5)
    rms = jnp.sqrt(squares / (valid_len.astype(F32)[:, None] * width))
    return (
        mixed_out[:, :tok_here], grad_x[:, :tok_here].astype(F32), rms, sums1[2], sums1[3], total_q, sums1[0], sums1[1],
        total_p.astype(F32), sums2[5], sums2[4], sums2[2], sums2[3], total_1.astype(F32), sums2[10:14].reshape(-1),
        total_2.astype(F32), sums2[1], sums2[0],
    )


def FWD_BLOCKS(rows):
    first = (rows // 2 + 15) // 16 * 16
    return (first, rows - first)


def solution(mesh):
    in_specs = (
        P("fsdp", "seq", None),
        P("fsdp"),
        P("fsdp", "seq", None),
        P("fsdp"),
        P("fsdp"),
        P("fsdp", None),
        P("fsdp"),
        P("fsdp"),
        P("fsdp", None),
        P("fsdp"),
        P("fsdp"),
        P("fsdp"),
        P("fsdp"),
        P("fsdp", None),
        P("fsdp"),
        P("fsdp", None),
        P("fsdp"),
        P("fsdp"),
    )
    out_specs = (
        P("fsdp", "seq", None),
        P("fsdp", "seq", None),
        P("fsdp", None),
        P("fsdp"),
        P("fsdp"),
        P("fsdp", None),
        P("fsdp"),
        P("fsdp"),
        P("fsdp", None),
        P("fsdp"),
        P("fsdp"),
        P("fsdp"),
        P("fsdp"),
        P("fsdp", None),
        P("fsdp"),
        P("fsdp", None),
        P("fsdp"),
        P("fsdp"),
    )
    seq_count = mesh.shape["seq"]
    paired = seq_count == 4 and mesh.shape["fsdp"] == 8
    return jax.shard_map(
        fast_device if paired else generic_device, mesh=mesh, in_specs=in_specs, out_specs=out_specs, check_vma=False
    )
```

```python
import functools

import jax
import jax.numpy as jnp
from jax import lax
from jax.experimental import pallas as pl
from jax.experimental.pallas import tpu as pltpu
from jax.sharding import PartitionSpec as P

EPSILON = 1e-06
HEAD_DIM = 64


def for_sending(value):
    return jax.tree.map(lambda a: a.astype(jnp.bfloat16) if a.dtype == jnp.float32 else a, value)


def layer_norm(values, gain, shift):
    average = jnp.mean(values, axis=-1, keepdims=True)
    centered = values - average
    variance = jnp.mean(centered * centered, axis=-1, keepdims=True)
    return centered * lax.rsqrt(variance + EPSILON) * gain + shift


def gelu_exact(values):
    return jax.nn.gelu(values, approximate=False)


def block_rows(length):
    return length // 2


def attend_image(inputs_one):
    queries, keys_in, values_in, length_one = inputs_one
    length = queries.shape[0]
    rows = block_rows(length)
    scaling = queries.shape[2] ** (-0.5)
    live_keys = (jnp.arange(length, dtype=jnp.int32) < length_one)[None, None, :]
    outputs = []
    totals = []
    for section in range(length // rows):
        part_q = queries[section * rows : (section + 1) * rows]
        scores = (
            jnp.einsum("qhe,khe->hqk", part_q, keys_in, preferred_element_type=jnp.float32)
            * scaling
        )
        scores = jnp.where(live_keys, scores, -1e30)
        highest = jnp.max(scores, axis=-1, keepdims=True)
        exponent = jnp.exp(scores - highest)
        row_sums = jnp.sum(exponent, axis=-1, keepdims=True)
        probabilities = (exponent / row_sums).astype(jnp.bfloat16)
        outputs.append(
            jnp.einsum("hqk,khe->qhe", probabilities, values_in, preferred_element_type=jnp.float32)
        )
        totals.append(highest + jnp.log(row_sums))
    return (jnp.concatenate(outputs, axis=0).astype(jnp.bfloat16), jnp.concatenate(totals, axis=1))


def attend_back(inputs_one):
    queries, keys_in, values_in, grad_out, log_total, length_one = inputs_one
    length = queries.shape[0]
    rows = block_rows(length)
    scaling = queries.shape[2] ** (-0.5)
    live_keys = (jnp.arange(length, dtype=jnp.int32) < length_one)[None, None, :]
    grad_keys = jnp.zeros(keys_in.shape, jnp.float32)
    grad_values = jnp.zeros(values_in.shape, jnp.float32)
    grad_queries = []
    for section in range(length // rows):
        part_q = queries[section * rows : (section + 1) * rows]
        part_grad = grad_out[section * rows : (section + 1) * rows]
        part_total = log_total[:, section * rows : (section + 1) * rows]
        scores = (
            jnp.einsum("qhe,khe->hqk", part_q, keys_in, preferred_element_type=jnp.float32)
            * scaling
        )
        scores = jnp.where(live_keys, scores, -1e30)
        probabilities = jnp.exp(scores - part_total)
        rounded = probabilities.astype(jnp.bfloat16)
        grad_prob = jnp.einsum(
            "qhe,khe->hqk", part_grad, values_in, preferred_element_type=jnp.float32
        )
        centre = jnp.sum(probabilities * grad_prob, axis=-1, keepdims=True)
        grad_scores = (probabilities * (grad_prob - centre)).astype(jnp.bfloat16)
        grad_queries.append(
            jnp.einsum("hqk,khe->qhe", grad_scores, keys_in, preferred_element_type=jnp.float32)
            * scaling
        )
        grad_keys = (
            grad_keys
            + jnp.einsum("hqk,qhe->khe", grad_scores, part_q, preferred_element_type=jnp.float32)
            * scaling
        )
        grad_values = grad_values + jnp.einsum(
            "hqk,qhe->khe", rounded, part_grad, preferred_element_type=jnp.float32
        )
    stacked = jnp.stack([jnp.concatenate(grad_queries, axis=0), grad_keys, grad_values], axis=1)
    return stacked.astype(jnp.bfloat16)


def generic_device(
    tokens,
    valid_len,
    cotangent,
    norm1_gain,
    norm1_shift,
    qkv_weight,
    query_bias,
    value_bias,
    proj_weight,
    proj_bias,
    attn_scale,
    norm2_gain,
    norm2_shift,
    fc1_weight,
    fc1_bias,
    fc2_weight,
    fc2_bias,
    mlp_scale,
):
    gathered = (
        lax.all_gather(norm1_gain, "fsdp", axis=0, tiled=True),
        lax.all_gather(norm1_shift, "fsdp", axis=0, tiled=True),
        lax.all_gather(qkv_weight, "fsdp", axis=0, tiled=True),
        lax.all_gather(query_bias, "fsdp", axis=0, tiled=True),
        lax.all_gather(value_bias, "fsdp", axis=0, tiled=True),
        lax.all_gather(proj_weight, "fsdp", axis=0, tiled=True),
        lax.all_gather(proj_bias, "fsdp", axis=0, tiled=True),
        lax.all_gather(attn_scale, "fsdp", axis=0, tiled=True),
        lax.all_gather(norm2_gain, "fsdp", axis=0, tiled=True),
        lax.all_gather(norm2_shift, "fsdp", axis=0, tiled=True),
        lax.all_gather(fc1_weight, "fsdp", axis=0, tiled=True),
        lax.all_gather(fc1_bias, "fsdp", axis=0, tiled=True),
        lax.all_gather(fc2_weight, "fsdp", axis=0, tiled=True),
        lax.all_gather(fc2_bias, "fsdp", axis=0, tiled=True),
        lax.all_gather(mlp_scale, "fsdp", axis=0, tiled=True),
    )
    (
        gain_one,
        shift_one,
        weight_qkv,
        bias_query,
        bias_value,
        weight_proj,
        bias_proj,
        scale_one,
        gain_two,
        shift_two,
        weight_up,
        bias_up,
        weight_down,
        bias_down,
        scale_two,
    ) = gathered
    images_here, tok_here, width = tokens.shape
    seq_count = lax.axis_size("seq")
    head_cols = width // seq_count
    heads_here = head_cols // HEAD_DIM
    length = tok_here * seq_count
    inputs_f = tokens.astype(jnp.float32)
    gain_first = gain_one.astype(jnp.float32)
    shift_first = shift_one.astype(jnp.float32)
    gain_second = gain_two.astype(jnp.float32)
    shift_second = shift_two.astype(jnp.float32)
    scale_first = scale_one.astype(jnp.float32)
    scale_second = scale_two.astype(jnp.float32)
    normed_first = layer_norm(inputs_f, gain_first, shift_first).astype(jnp.bfloat16)
    bias_all = jnp.concatenate(
        [
            bias_query.astype(jnp.float32),
            jnp.zeros((width,), jnp.float32),
            bias_value.astype(jnp.float32),
        ]
    )
    projected = (
        jnp.einsum("mtd,de->mte", normed_first, weight_qkv, preferred_element_type=jnp.float32)
        + bias_all
    ).astype(jnp.bfloat16)
    by_heads = lax.all_to_all(
        projected.reshape(images_here, tok_here, 3, seq_count, head_cols),
        "seq",
        split_axis=3,
        concat_axis=1,
        tiled=True,
    )
    by_heads = by_heads.reshape(images_here, length, 3, heads_here, HEAD_DIM)
    attended, log_total = lax.map(
        attend_image, (by_heads[:, :, 0], by_heads[:, :, 1], by_heads[:, :, 2], valid_len)
    )
    attended_tok = lax.all_to_all(
        for_sending(attended.reshape(images_here, length, 1, head_cols)),
        "seq",
        split_axis=1,
        concat_axis=2,
        tiled=True,
    )
    attended_tok = attended_tok.reshape(images_here, tok_here, width)
    attn_out = jnp.einsum(
        "mtd,de->mte", attended_tok, weight_proj, preferred_element_type=jnp.float32
    ) + bias_proj.astype(jnp.float32)
    branch_attn = scale_first * attn_out
    middle = inputs_f + branch_attn
    normed_second = layer_norm(middle, gain_second, shift_second).astype(jnp.bfloat16)
    hidden_pre = jnp.einsum(
        "mtd,df->mtf", normed_second, weight_up, preferred_element_type=jnp.float32
    ) + bias_up.astype(jnp.float32)
    hidden = gelu_exact(hidden_pre).astype(jnp.bfloat16)
    mlp_out = jnp.einsum(
        "mtf,fd->mtd", hidden, weight_down, preferred_element_type=jnp.float32
    ) + bias_down.astype(jnp.float32)
    branch_mlp = scale_second * mlp_out
    result = middle + branch_mlp
    positions = lax.axis_index("seq") * tok_here + jnp.arange(tok_here, dtype=jnp.int32)
    live = (positions[None, :] < valid_len[:, None]).astype(jnp.float32)[:, :, None]
    squares = jnp.stack(
        [
            jnp.sum(live * piece * piece, axis=(1, 2))
            for piece in (inputs_f, branch_attn, middle, branch_mlp, result)
        ],
        axis=-1,
    )
    squares = lax.psum(squares, "seq")
    rms_stats = jnp.sqrt(squares / (valid_len.astype(jnp.float32)[:, None] * width))
    grad_result = cotangent.astype(jnp.float32)
    grad_mlp_scale = jnp.sum(grad_result * mlp_out, axis=(0, 1))
    grad_mlp_out = (grad_result * scale_second).astype(jnp.bfloat16)
    grad_fc2_bias = jnp.sum(grad_mlp_out, axis=(0, 1), dtype=jnp.float32)
    grad_fc2_weight = jnp.einsum(
        "mtf,mtd->fd", hidden, grad_mlp_out, preferred_element_type=jnp.float32
    )
    grad_hidden = jnp.einsum(
        "mtd,fd->mtf", grad_mlp_out, weight_down, preferred_element_type=jnp.float32
    )
    gelu_value, gelu_back = jax.vjp(gelu_exact, hidden_pre)
    grad_pre = gelu_back(grad_hidden)[0].astype(jnp.bfloat16)
    grad_fc1_bias = jnp.sum(grad_pre, axis=(0, 1), dtype=jnp.float32)
    grad_fc1_weight = jnp.einsum(
        "mtd,mtf->df", normed_second, grad_pre, preferred_element_type=jnp.float32
    )
    grad_normed_second = jnp.einsum(
        "mtf,df->mtd", grad_pre, weight_up, preferred_element_type=jnp.float32
    )
    norm_value, norm_back = jax.vjp(layer_norm, middle, gain_second, shift_second)
    grad_middle_norm, grad_norm2_gain, grad_norm2_shift = norm_back(grad_normed_second)
    grad_middle = grad_result + grad_middle_norm
    grad_attn_scale = jnp.sum(grad_middle * attn_out, axis=(0, 1))
    grad_attn_out = (grad_middle * scale_first).astype(jnp.bfloat16)
    grad_proj_bias = jnp.sum(grad_attn_out, axis=(0, 1), dtype=jnp.float32)
    grad_proj_weight = jnp.einsum(
        "mtd,mte->de", attended_tok, grad_attn_out, preferred_element_type=jnp.float32
    )
    grad_attended = jnp.einsum(
        "mte,de->mtd", grad_attn_out, weight_proj, preferred_element_type=jnp.float32
    ).astype(jnp.bfloat16)
    grad_heads = lax.all_to_all(
        grad_attended.reshape(images_here, tok_here, seq_count, head_cols),
        "seq",
        split_axis=2,
        concat_axis=1,
        tiled=True,
    )
    grad_heads = grad_heads.reshape(images_here, length, heads_here, HEAD_DIM)
    grad_qkv = lax.map(
        attend_back,
        (by_heads[:, :, 0], by_heads[:, :, 1], by_heads[:, :, 2], grad_heads, log_total, valid_len),
    )
    grad_projected = lax.all_to_all(
        for_sending(grad_qkv.reshape(images_here, length, 3, 1, head_cols)),
        "seq",
        split_axis=1,
        concat_axis=3,
        tiled=True,
    )
    grad_projected = grad_projected.reshape(images_here, tok_here, 3 * width)
    grad_query_bias = jnp.sum(grad_projected[:, :, :width], axis=(0, 1), dtype=jnp.float32)
    grad_value_bias = jnp.sum(grad_projected[:, :, 2 * width :], axis=(0, 1), dtype=jnp.float32)
    grad_qkv_weight = jnp.einsum(
        "mtd,mte->de", normed_first, grad_projected, preferred_element_type=jnp.float32
    )
    grad_normed_first = jnp.einsum(
        "mte,de->mtd", grad_projected, weight_qkv, preferred_element_type=jnp.float32
    )
    first_value, first_back = jax.vjp(layer_norm, inputs_f, gain_first, shift_first)
    grad_input_norm, grad_norm1_gain, grad_norm1_shift = first_back(grad_normed_first)
    input_grad = grad_middle + grad_input_norm
    reduced = (
        lax.psum_scatter(grad_norm1_gain, "fsdp", scatter_dimension=0, tiled=True),
        lax.psum_scatter(grad_norm1_shift, "fsdp", scatter_dimension=0, tiled=True),
        lax.psum_scatter(grad_qkv_weight, "fsdp", scatter_dimension=0, tiled=True),
        lax.psum_scatter(grad_query_bias, "fsdp", scatter_dimension=0, tiled=True),
        lax.psum_scatter(grad_value_bias, "fsdp", scatter_dimension=0, tiled=True),
        lax.psum_scatter(grad_proj_weight, "fsdp", scatter_dimension=0, tiled=True),
        lax.psum_scatter(grad_proj_bias, "fsdp", scatter_dimension=0, tiled=True),
        lax.psum_scatter(grad_attn_scale, "fsdp", scatter_dimension=0, tiled=True),
        lax.psum_scatter(grad_norm2_gain, "fsdp", scatter_dimension=0, tiled=True),
        lax.psum_scatter(grad_norm2_shift, "fsdp", scatter_dimension=0, tiled=True),
        lax.psum_scatter(grad_fc1_weight, "fsdp", scatter_dimension=0, tiled=True),
        lax.psum_scatter(grad_fc1_bias, "fsdp", scatter_dimension=0, tiled=True),
        lax.psum_scatter(grad_fc2_weight, "fsdp", scatter_dimension=0, tiled=True),
        lax.psum_scatter(grad_fc2_bias, "fsdp", scatter_dimension=0, tiled=True),
        lax.psum_scatter(grad_mlp_scale, "fsdp", scatter_dimension=0, tiled=True),
    )
    reduced = lax.psum(
        (
            reduced[0],
            reduced[1],
            reduced[2],
            reduced[3],
            reduced[4],
            reduced[5],
            reduced[6],
            reduced[7],
            reduced[8],
            reduced[9],
            reduced[10],
            reduced[11],
            reduced[12],
            reduced[13],
            reduced[14],
        ),
        "seq",
    )
    return (
        result.astype(jnp.bfloat16),
        input_grad,
        rms_stats,
        reduced[0],
        reduced[1],
        reduced[2],
        reduced[3],
        reduced[4],
        reduced[5],
        reduced[6],
        reduced[7],
        reduced[8],
        reduced[9],
        reduced[10],
        reduced[11],
        reduced[12],
        reduced[13],
        reduced[14],
    )


NT = (((1,), (1,)), ((), ()))
NN = (((1,), (0,)), ((), ()))
TN = (((0,), (0,)), ((), ()))

def dotf(a, b, dims):
    return lax.dot_general(a, b, dims, preferred_element_type=jnp.float32)

F32 = jnp.float32
BF = jnp.bfloat16

def norm_parts(v):
    mean = jnp.mean(v, axis=-1, keepdims=True)
    cen = v - mean
    var = jnp.mean(cen * cen, axis=-1, keepdims=True)
    r = lax.rsqrt(var + EPSILON)
    return cen * r, r

def norm_back(z, r, grad, gain):
    e = grad * gain
    return r * (e - jnp.mean(e, axis=-1, keepdims=True) - z * jnp.mean(e * z, axis=-1, keepdims=True))

MESH = pl.DeviceIdType.MESH


def places():
    f = lax.axis_index("fsdp")
    z = lax.axis_index("seq")
    core = f % 2
    dx = 2 - 4 * (f // 2 % 2)
    dy = 4 - 8 * (f // 4)
    da = (1 - core) * dx + core * dy
    db = core * dx + (1 - core) * dy
    mate = f + 1 - 2 * core
    return f, z, mate, da, db


def chip_scratch(rows, cols, chunks, kind):
    dma = pltpu.SemaphoreType.DMA
    return [pltpu.VMEM((n, rows, cols), kind) for n in (4, 3)] + [dma((chunks, n)) for n in (4, 4, 3, 3, 4)]


def line_scratch(rows, cols, chunks, kind):
    dma = pltpu.SemaphoreType.DMA
    return [pltpu.VMEM((2, rows, cols), kind), pltpu.VMEM((rows, cols), kind), dma((chunks, 2)), dma((chunks, 2))]


def reduce_scratch(rows, cols, chunks, kind):
    return chip_scratch(rows, cols, 1, kind) + line_scratch(rows, cols, chunks, kind)


CHIP_REFS = 7
LINE_REFS = 4


def remote(a, b, s, r, dev):
    return pltpu.make_async_remote_copy(src_ref=a, dst_ref=b, send_sem=s, recv_sem=r, device_id=dev, device_id_type=MESH)


def chip_steps(src, tot, scratch, cuts, mine=None):
    yours, came, ex_send, ex_recv, l_send, l_recv, load_sem = scratch
    f, z, mate, da, db = places()
    own = (f + da + db, f + db, f + da, f)
    other = (mate + da + db, mate + da, mate + db, mate)

    def steps(k, lo, size):
        at = pl.ds(lo, size)

        def load(m):
            return pltpu.make_async_copy(src.at[own[m], at], mine.at[m, at], load_sem.at[k, m])

        def swap(m):
            return remote(src.at[other[m], at], yours.at[m, at], ex_send.at[k, m], ex_recv.at[k, m], (mate, z))

        def hop(i):
            return remote(
                yours.at[i, at], came.at[i, at], l_send.at[k, i], l_recv.at[k, i], (f + (da if i == 2 else db), z)
            )

        def merge(m):
            swap(m).wait_recv()
            if mine is None:
                yours[m, at] = yours[m, at] + src[own[m], at]
            else:
                load(m).wait()
                yours[m, at] = yours[m, at] + mine[m, at]

        def s0():
            for m in range(4):
                swap(m).start()
                if mine is not None:
                    load(m).start()

        def s1():
            for m in range(2):
                merge(m)
                hop(m).start()

        def s2():
            merge(2)
            merge(3)
            hop(0).wait_recv()
            yours[2, at] = yours[2, at] + came[0, at]
            hop(2).start()

        def s3():
            hop(1).wait_recv()
            hop(2).wait_recv()
            total = yours[3, at].astype(F32) + came[1, at].astype(F32) + came[2, at].astype(F32)
            tot[at] = total.astype(tot.dtype)

        def s4():
            for m in range(4):
                swap(m).wait_send()
            for i in range(3):
                hop(i).wait_send()

        return [s0, s1, s2, s3, s4]

    return [steps(k, lo, size) for k, (lo, size) in enumerate(cuts)]


def line_steps(first, out, scratch, cuts):
    zin, tot, z_send, z_recv = scratch
    f, z, _mate, _da, _db = places()
    outer = z % 3 == 0
    inner = z % 3 != 0

    def steps(k, lo, size):
        at = pl.ds(lo, size)

        def to_inner():
            return remote(tot.at[at], zin.at[0, at], z_send.at[k, 0], z_recv.at[k, 0], (f, 1 + z // 3))

        def across():
            return remote(tot.at[at], zin.at[1, at], z_send.at[k, 0], z_recv.at[k, 1], (f, 3 - z))

        def to_outer():
            return remote(out.at[at], zin.at[1, at], z_send.at[k, 1], z_recv.at[k, 1], (f, 3 * (z - 1)))

        def s0():
            if first is not None:
                tot[at] = first[at]

            @pl.when(outer)
            def _():
                to_inner().start()

        def s1():
            @pl.when(inner)
            def _():
                to_inner().wait_recv()
                tot[at] = tot[at] + zin[0, at]
                across().start()

        def s2():
            @pl.when(inner)
            def _():
                across().wait_recv()
                out[at] = tot[at] + zin[1, at]
                to_outer().start()

        def s3():
            @pl.when(outer)
            def _():
                to_outer().wait_recv()
                out[at] = zin[1, at]
                to_inner().wait_send()

            @pl.when(inner)
            def _():
                across().wait_send()
                to_outer().wait_send()

        return [s0, s1, s2, s3]

    return [steps(k, lo, size) for k, (lo, size) in enumerate(cuts)]


def line_waves(lines):
    def wave(w):
        def run():
            for i in range(3):
                if 0 <= w - i < len(lines):
                    lines[w - i][1 + i]()

        return run

    return [wave(w) for w in range(len(lines) + 2)]


def reduce_steps(src, out, scratch, cuts, mine=None):
    line = scratch[CHIP_REFS:]
    (chip,) = chip_steps(src, line[1], scratch[:CHIP_REFS], [(0, out.shape[0])], mine)
    lines = line_steps(None, out, line, cuts)

    def both(*todo):
        def run():
            for step in todo:
                step()

        return run

    waves = line_waves(lines)
    return [chip[:3] + [both(chip[3], *(l[0] for l in lines))] + waves[:-1] + [both(waves[-1], chip[4])]]


REDUCE_REFS = CHIP_REFS + LINE_REFS


def timetable(starts, offsets, every):
    return sorted(
        (at + offsets[i], k, i) for k, at in enumerate(starts) for i, step in enumerate(every[k])
        if step is not None and offsets[i] is not None
    )


def run_steps(every, table, lo, hi):
    for at, k, i in table:
        if lo <= at < hi:
            every[k][i]()


FOREVER = 10**6


def even_cuts(rows, parts):
    size = rows // parts // 16 * 16
    cuts = [(i * size, size) for i in range(parts - 1)]
    return cuts + [((parts - 1) * size, rows - (parts - 1) * size)]


def relay_partner(f, z, turn):
    return f - f % 2 + z // 2, 2 * (f % 2) + (z + turn) % 2


def greet(relay, line=True):
    f, z, mate, da, db = places()
    barrier = pltpu.get_barrier_semaphore()

    def signal(group, place):
        pl.semaphore_signal(barrier, inc=1, device_id=(group, place), device_id_type=MESH)

    for other in (mate, f + da, f + db):
        signal(other, z)

    if line:
        @pl.when(z > 0)
        def _():
            signal(f, z - 1)

        @pl.when(z < 3)
        def _():
            signal(f, z + 1)

    if relay:
        signal(*relay_partner(f, z, 1))

        @pl.when(z // 2 != f % 2)
        def _():
            signal(*relay_partner(f, z, 0))

    away = z // 2 - f % 2
    count = 4 + (z + 2) // 3 - z // 3 if line else 3
    pl.semaphore_wait(barrier, count + 1 + away * away if relay else count)


def relay_steps(src, out, sems, outward=False):
    f, z, _mate, _da, _db = places()
    here = z // 2 == f % 2

    def ends(turn):
        return (src.at[(z + turn) % 2], out.at[turn]) if outward else (src.at[turn], out.at[z % 2])

    def copy(turn):
        a, b = ends(turn)
        return pltpu.make_async_remote_copy(
            src_ref=a, dst_ref=b, send_sem=sems.at[turn], recv_sem=sems.at[2 + turn],
            device_id=relay_partner(f, z, turn), device_id_type=MESH)

    def local():
        a, b = ends(0)
        return pltpu.make_async_copy(a, b, sems.at[0])

    def start():
        copy(1).start()

        @pl.when(here)
        def _():
            local().start()

        @pl.when(jnp.logical_not(here))
        def _():
            copy(0).start()

    def wait():
        copy(1).wait()

        @pl.when(here)
        def _():
            local().wait()

        @pl.when(jnp.logical_not(here))
        def _():
            copy(0).wait()

    return start, wait


def gather_scratch(chunks):
    dma = pltpu.SemaphoreType.DMA
    return [dma((chunks, 7)), dma((chunks, 7)), dma((chunks,))]


def gather_steps(own, full, sems, cuts):
    send, recv, local_sem = sems
    f, z, mate, da, db = places()

    def steps(k, lo, size):
        at = pl.ds(lo, size)

        def copy(i, src, slot, dev):
            return pltpu.make_async_remote_copy(
                src_ref=src, dst_ref=full.at[slot, at], send_sem=send.at[k, i], recv_sem=recv.at[k, i],
                device_id=(dev, z), device_id_type=MESH)

        mine = own.at[at]

        def sent(i):
            slot = (f, f, f, f + da, f + da, f + db, f + da + db)[i]
            dev = (f + da, f + db, mate, f + db, mate, mate, mate)[i]
            return copy(i, mine if i < 3 else full.at[slot, at], slot, dev)

        def came(i):
            slot = (f + da, f + db, mate, f + da + db, mate + db, mate + da, mate + da + db)[i]
            return copy(i, mine, slot, mate)

        def local():
            return pltpu.make_async_copy(mine, full.at[f, at], local_sem.at[k])

        def g0():
            for i in range(3):
                sent(i).start()
            local().start()

        def g1():
            came(0).wait_recv()
            sent(3).start()
            sent(4).start()
            came(1).wait_recv()
            sent(5).start()

        def g2():
            came(3).wait_recv()
            sent(6).start()

        def g3():
            for i in (2, 4, 5, 6):
                came(i).wait_recv()
            local().wait()
            for i in range(7):
                sent(i).wait_send()

        return [g0, g1, g2, g3]

    return [steps(k, lo, size) for k, (lo, size) in enumerate(cuts)]


FIRST_QUARTERS = 2


def gather_quarters(w1_own, w2_own, w1_full, w2_full, sems, first, count):
    rows = w1_own.shape[1]
    every = []
    for i in range(count):
        pairs = ((w1_own.at[first + i], w1_full.at[i]), (w2_own.at[pl.ds((first + i) * rows, rows)], w2_full.at[i]))
        for j, (own, full) in enumerate(pairs):
            at = 3 * (2 * i + j)
            every += gather_steps(own, full, sems[at:at + 3], [(0, rows)])
    return every


def run_gather(every):
    for s in range(1, 4):
        for c in every:
            c[s]()


def qkv_kernel(cuts, tok_ref, own_small, wq_own, wp_own, w1_own,
               x_ref, nt_ref, q_ref, kv_ref, kv_other, wq_out, wp_out, vec_ref, mask_ref, w1_cut,
               small, xs, wq, kv_sems, out_sem, relay_sems, cut_sems, *sems):
    f, z, mate, _da, _db = places()
    tok = xs.shape[1]
    rows, width = x_ref.shape
    greet(True, False)
    relay_start, relay_wait = relay_steps(tok_ref, xs, relay_sems, True)
    relay_start()
    lists = [
        gather_steps(own, full, sems[3 * i:3 * i + 3], cut)
        for i, (own, full, cut) in enumerate(((own_small, small, cuts[0]), (wq_own, wq, cuts[1]), (wp_own, wp_out, cuts[2])))
    ]
    every = lists[0] + lists[1]
    for c in every:
        c[0]()
    slabs = w1_cut.shape[2] // 128
    moves = []
    for i in range(slabs):
        for quarter in range(4):
            moves.append(pltpu.make_async_copy(
                w1_own.at[:, pl.ds((4 * i + quarter) * 128, 128)], w1_cut.at[quarter, :, pl.ds(i * 128, 128)],
                cut_sems.at[i, quarter]))
    for move in moves:
        move.start()
    run_gather(lists[0])
    part = small.shape[2]
    for i in range(small.shape[0]):
        vec_ref[:, i * part:(i + 1) * part] = small[i]
    lane = lax.broadcasted_iota(jnp.int32, (1, part), 1)
    line = small[f // 2 * 2 + z // 2, 14:15, :]
    length = jnp.sum(jnp.where(lane == z % 2, line, 0.0), axis=1, keepdims=True)
    lanes = lax.broadcasted_iota(jnp.int32, (rows, 128), 1)
    at = lax.broadcasted_iota(jnp.int32, (rows, 128), 0)
    ones = jnp.where(lanes < 4, 1.0, 0.0)
    for i in range(2):
        core = f % 2 if i == 0 else 1 - f % 2
        first = tok * (2 * core + z % 2)
        second = tok * (2 * core + (z + 1) % 2) - tok
        pos = (at + jnp.where(at < tok, first, second)).astype(F32)
        masked = jnp.where(pos < length, 0.0, -1e30)
        mask_ref[i * rows:(i + 1) * rows, :] = jnp.where(lanes == 0, masked, ones).astype(BF)
    for c in lists[1]:
        c[1]()
    for c in lists[2]:
        c[0]()
    relay_wait()
    x = jnp.concatenate([xs[0].astype(F32), xs[1].astype(F32)], axis=0)
    x_ref[...] = x.astype(BF)
    zn, _r = norm_parts(x)
    n = (zn * vec_ref[0:1, :] + vec_ref[1:2, :]).astype(BF)
    for s in (2, 3):
        for c in lists[1]:
            c[s]()
    keep = pltpu.make_async_copy(wq, wq_out, out_sem)
    keep.start()

    def give(i):
        return pltpu.make_async_remote_copy(
            src_ref=kv_ref.at[i], dst_ref=kv_other.at[i], send_sem=kv_sems.at[i], recv_sem=kv_sems.at[2 + i],
            device_id=(mate, z), device_id_type=MESH)

    def product(i):
        w = wq[:, :, i * width:(i + 1) * width].reshape(width, width)
        return dotf(n, w, NN)

    kv_ref[0] = product(1).astype(BF)
    give(0).start()
    kv_ref[1] = (product(2) + vec_ref[3:4, :]).astype(BF)
    give(1).start()
    for c in lists[2]:
        c[1]()
    q_ref[...] = (product(0) + vec_ref[2:3, :]).astype(BF) * jnp.asarray(0.125, BF)
    nt_ref[...] = n.T
    for s in (2, 3):
        for c in lists[2]:
            c[s]()
    for i in range(2):
        give(i).wait()
    keep.wait()
    for move in moves:
        move.wait()


def qkv(tokens, small, wq, wp, w1, groups):
    width = tokens.shape[2]
    tok = tokens.shape[1]
    rows = 2 * tok
    sd = jax.ShapeDtypeStruct
    hbm = pl.BlockSpec(memory_space=pltpu.HBM)
    vmem = pl.BlockSpec(memory_space=pltpu.VMEM)
    cuts = [[(0, small.shape[0])], even_cuts(wq.shape[0], 4), even_cuts(wp.shape[0], 2)]
    dma = pltpu.SemaphoreType.DMA
    sems = []
    for cut in cuts:
        sems += gather_scratch(len(cut))
    return pl.pallas_call(
        functools.partial(qkv_kernel, cuts),
        in_specs=[hbm, vmem, hbm, hbm, hbm],
        out_specs=[vmem, vmem, vmem, vmem, hbm, hbm, hbm, vmem, vmem, hbm],
        out_shape=[sd((rows, width), BF), sd((width, rows), BF), sd((rows, width), BF), sd((2, rows, width), BF), sd((2, rows, width), BF),
            sd((groups,) + wq.shape, BF), sd((groups,) + wp.shape, BF), sd((small.shape[0], width), F32), sd((2 * rows, 128), BF),
            sd((4, w1.shape[0], w1.shape[1] // 4), BF)],
        scratch_shapes=[pltpu.VMEM((groups,) + small.shape, F32), pltpu.VMEM((2, tok, width), BF), pltpu.VMEM((groups,) + wq.shape, BF),
            dma((4,)), dma(()), dma((4,)), dma((w1.shape[1] // 512, 4))] + sems,
        compiler_params=pltpu.CompilerParams(vmem_limit_bytes=60 * 2**20, collective_id=3, has_side_effects=True), name="qkv",
    )(tokens, small, wq, wp, w1)


def att_fwd_kernel(blocks, q_ref, ko_ref, kp_ref, vo_ref, vp_ref, bias_ref, cot_ref, w1_own, w2_own,
                   o_ref, st_ref, cot_out, w1_out, w2_out, kbuf, vbuf, relay_sems, *sems):
    rows = q_ref.shape[0]
    step = pl.program_id(0)
    every = gather_quarters(w1_own, w2_own, w1_out, w2_out, sems, 0, w1_out.shape[0])
    relay_start, relay_wait = relay_steps(cot_ref, cot_out, relay_sems, True)

    @pl.when(step == 0)
    def _():
        greet(True, False)
        relay_start()
        for c in every:
            c[0]()
        kbuf[:, 128:] = bias_ref[...]
        vbuf[:, 128:] = jnp.ones_like(vbuf[:, 128:])

    kbuf[:rows, :128] = ko_ref[0]
    kbuf[rows:, :128] = kp_ref[0]
    vbuf[:rows, :128] = vo_ref[0]
    vbuf[rows:, :128] = vp_ref[0]
    start = 0
    for size in blocks:
        lane = lax.broadcasted_iota(jnp.int32, (size, 128), 1)
        low = lane < 64
        first = (lane == 0).astype(jnp.bfloat16)
        q = q_ref[start:start + size, :]
        heads = []
        for h in range(2):
            keep = low if h == 0 else jnp.logical_not(low)
            qm = jnp.where(keep, q, jnp.zeros_like(q))
            qx = jnp.concatenate([qm, first], axis=1)
            s = dotf(qx, kbuf[...], NT)
            m = jnp.max(s, axis=-1, keepdims=True)
            p = jnp.exp(s - m).astype(jnp.bfloat16)
            ol = dotf(p, vbuf[...], NN)
            l = ol[:, 128:]
            heads.append(ol[:, :128] / l)
            total = -(m + jnp.log(l))
            hi = total.astype(jnp.bfloat16).astype(jnp.float32)
            mid = (total - hi).astype(jnp.bfloat16).astype(jnp.float32)
            lo = total - hi - mid
            piece = jnp.where(lane == 0, 1.0, jnp.where(lane == 1, hi, jnp.where(lane == 2, mid, jnp.where(lane == 3, lo, 0.0))))
            st_ref[h, start:start + size, :] = piece.astype(jnp.bfloat16)
        o_ref[start:start + size, :] = jnp.where(low, heads[0], heads[1]).astype(jnp.bfloat16)
        start += size

    @pl.when(step == pl.num_programs(0) - 1)
    def _():
        run_gather(every)
        relay_wait()


def att_fwd(q, kv_own, kv_other, bias, blocks, cot, w1, w2, groups):
    rows, width = q.shape
    pairs = width // 128
    heads = width // 64
    hbm = pl.BlockSpec(memory_space=pltpu.HBM)
    key = pl.BlockSpec((1, rows, 128), lambda i: (0, 0, i))
    val = pl.BlockSpec((1, rows, 128), lambda i: (1, 0, i))
    sd = jax.ShapeDtypeStruct
    sems = gather_scratch(1) * (2 * FIRST_QUARTERS)
    full = sd((FIRST_QUARTERS, groups) + w1.shape[1:], BF)
    return pl.pallas_call(
        functools.partial(att_fwd_kernel, blocks),
        grid=(pairs,),
        in_specs=[pl.BlockSpec((rows, 128), lambda i: (0, i)), key, key, val, val, pl.BlockSpec((2 * rows, 128), lambda i: (0, 0)),
            hbm, hbm, hbm],
        out_specs=[pl.BlockSpec((rows, 128), lambda i: (0, i)), pl.BlockSpec((2, rows, 128), lambda i: (i, 0, 0)), hbm, hbm, hbm],
        out_shape=[sd((rows, width), BF), sd((heads, rows, 128), BF), sd(cot.shape, BF), full, full],
        scratch_shapes=[pltpu.VMEM((2 * rows, 256), BF), pltpu.VMEM((2 * rows, 256), BF), pltpu.SemaphoreType.DMA((4,))] + sems,
        compiler_params=pltpu.CompilerParams(vmem_limit_bytes=56 * 2**20, collective_id=4, has_side_effects=True),
        name="att_fwd",
    )(q, kv_own, kv_other, kv_own, kv_other, bias, cot, w1, w2)


def mlp_kernel(starts, att_ref, x_ref, cot_ref, mask_ref, vec_ref, wp_ref, w1a, w2a, w1_own, w2_own,
               mixed_out, gmid_out, gatt_out, dwp_out, small_ref, w1b, w2b, dw1, dw2, *rest):
    units = len(starts)
    outs, (mid_ref, mixed, ao, n2, n2t, gm, acc, gn2, wb1, wb2, sb1, sb2, mine, w_sem, s_sem, o_sem) = rest[:units], rest[units:units + 16]
    rest = rest[units + 16:]
    step = pl.program_id(0)
    last = pl.num_programs(0) - 1
    part = att_ref.shape[1] // small_ref.shape[0]
    half = att_ref.shape[0] // 2
    fc = wb1.shape[3]
    late = w1b.shape[0]
    early = w1a.shape[0]
    gathers = gather_quarters(w1_own, w2_own, w1b, w2b, rest[:6 * late], early, late)
    rest = rest[6 * late:]
    sums = []
    for i in range(units):
        refs = rest[CHIP_REFS * i:CHIP_REFS * (i + 1)]
        sums += chip_steps((dw1, dw2)[i % 2].at[i // 2], outs[i], refs, [(0, part)], mine.at[i % 2])
    table = timetable(starts, (0, 1, 3, 4, 5), sums)
    cot = lambda: jnp.concatenate([cot_ref[0].astype(F32), cot_ref[1].astype(F32)], axis=0)
    col = lambda v: jnp.sum(v, axis=0, keepdims=True)

    def fetch(chunk, w1, w2, quarter):
        side = chunk % 2
        return (
            pltpu.make_async_copy(w1.at[quarter, :, :, pl.ds(pl.multiple_of(side * fc, fc), fc)], wb1.at[side], w_sem.at[side, 0]),
            pltpu.make_async_copy(w2.at[quarter, pl.ds(side * wb2.shape[1], wb2.shape[1])], wb2.at[side], w_sem.at[side, 1]),
        )

    def fetch_start(chunk):
        @pl.when(chunk // 2 < early)
        def _():
            for c in fetch(chunk, w1a, w2a, jnp.minimum(chunk // 2, early - 1)):
                c.start()

        @pl.when(chunk // 2 >= early)
        def _():
            for c in fetch(chunk, w1b, w2b, jnp.maximum(chunk // 2 - early, 0)):
                c.start()

    def store(chunk):
        side = chunk % 2
        return (
            pltpu.make_async_copy(sb1.at[side], dw1.at[chunk // 2, :, :, pl.ds(pl.multiple_of(side * fc, fc), fc)], s_sem.at[side, 0]),
            pltpu.make_async_copy(sb2.at[side], dw2.at[chunk // 2, pl.ds(side * wb2.shape[1], wb2.shape[1])], s_sem.at[side, 1]),
        )

    @pl.when(step == 0)
    def _():
        greet(False, False)
        for i in range(2):
            gathers[i][0]()
        fetch_start(0)
        a = dotf(att_ref[...], wp_ref[...], NN) + vec_ref[4:5, :]
        ao[...] = a
        mid = x_ref[...].astype(F32) + vec_ref[5:6, :] * a
        mid_ref[...] = mid
        zn, _r = norm_parts(mid)
        n = (zn * vec_ref[6:7, :] + vec_ref[7:8, :]).astype(BF)
        n2[...] = n
        n2t[...] = n.T
        gm[...] = (cot() * vec_ref[9:10, :]).astype(BF)
        acc[...] = jnp.broadcast_to(vec_ref[8:9, :], acc.shape)
        gn2[...] = jnp.zeros_like(gn2)
        small_ref[...] = jnp.zeros_like(small_ref)

    for c in fetch(step, w1a, w2a, 0):
        c.wait()

    for at in range(2 * 4):
        @pl.when(step == at)
        def _(at=at):
            for i in range(late):
                two = gathers[2 * i:2 * i + 2]
                for s in range(4):
                    if at == 2 * i + s and at > 0:
                        for g in two:
                            g[s]()

    @pl.when(step < last)
    def _():
        fetch_start(step + 1)

    side = step % 2
    w1 = wb1[side].reshape(wb1.shape[1] * wb1.shape[2], fc)
    w2 = wb2[side].reshape(fc, wb2.shape[3])
    b1 = vec_ref[pl.ds(10 + step // 2, 1), pl.ds(pl.multiple_of(side * fc, fc), fc)]
    u = dotf(n2[...], w1, NN) + b1
    phi = 0.5 + 0.5 * lax.erf(u * 0.7071067811865476)
    hid = (u * phi).astype(BF)
    slope = phi + u * jnp.exp(u * u * -0.5) * 0.3989422804014327
    gh = dotf(gm[...], w2, NT)
    gp = (gh * slope).astype(BF)
    gb1 = col(gp.astype(F32))
    for i in range(fc // part):
        small_ref[side * (fc // part) + i, pl.ds(10 + step // 2, 1), :] = gb1[:, i * part:(i + 1) * part]
    acc[...] += dotf(hid, w2, NN)
    gn2[...] += dotf(gp, w1, NT)
    sb2[side] = dotf(hid, gm[...], TN).astype(BF).reshape(sb2.shape[1:])
    sb1[side] = dotf(n2t[...], gp, NN).astype(BF).reshape(sb1.shape[1:])
    for c in store(step):
        c.start()

    @pl.when(step > 0)
    def _():
        for c in store(step - 1):
            c.wait()

    for at in range(2, 7):
        @pl.when(step == at)
        def _(at=at):
            run_steps(sums, table, at, at + 1)

    @pl.when(step == last)
    def _():
        def put(row, v):
            for i in range(small_ref.shape[0]):
                small_ref[i, row:row + 1, :] = v[:, i * part:(i + 1) * part]

        def write(a, b, i):
            return pltpu.make_async_copy(a, b, o_sem.at[i])

        out = acc[...]
        live = jnp.where(mask_ref[:, :1].astype(F32) < 0.0, 0.0, 1.0)
        x = x_ref[...].astype(F32)
        mid = mid_ref[...]
        branch = vec_ref[9:10, :] * out
        res = mid + branch
        mixed[0, :half] = res[:half].astype(BF)
        mixed[1, :half] = res[half:].astype(BF)
        mixed[:, half:] = jnp.zeros_like(mixed[:, half:])
        write(mixed, mixed_out, 0).start()
        put(0, col(cot() * out))
        put(1, col(gm[...].astype(F32)))
        ba = vec_ref[5:6, :] * ao[...]
        place = lax.axis_index("seq")
        owner = lax.axis_index("fsdp") // 2 * 2 + place // 2
        lane = lax.broadcasted_iota(jnp.int32, (1, part), 1)
        line = jnp.zeros((1, part), F32)
        for i, v in enumerate((x, ba, mid, branch, res)):
            line = jnp.where(lane == place % 2 * 5 + i, jnp.sum(col(live * v * v), axis=1, keepdims=True), line)
        for i in range(small_ref.shape[0]):
            small_ref[i, 14:15, :] = jnp.where(owner == i, line, 0.0)
        zn, r = norm_parts(mid)
        g = gn2[...]
        put(2, col(g * zn))
        put(3, col(g))
        gmid = cot() + norm_back(zn, r, g, vec_ref[6:7, :])
        mid_ref[...] = gmid
        write(mid_ref, gmid_out, 1).start()
        put(4, col(gmid * ao[...]))
        gao = (gmid * vec_ref[5:6, :]).astype(BF)
        put(5, col(gao.astype(F32)))
        n2[...] = dotf(gao, wp_ref[...], NT).astype(BF)
        write(n2, gatt_out, 2).start()
        run_steps(sums, table, 7, 8)
        wb2[...] = dotf(att_ref[...], gao, TN).astype(BF).reshape(wb2.shape)
        write(wb2, dwp_out, 3).start()
        run_steps(sums, table, 8, FOREVER)
        for i, (a, b) in enumerate(((mixed, mixed_out), (mid_ref, gmid_out), (n2, gatt_out), (wb2, dwp_out))):
            write(a, b, i).wait()
        for c in store(step):
            c.wait()


MLP_STARTS = (2, 3, 5)


def mlp(att, x, cot, mask, vec, wp, w1a, w2a, w1_own, w2_own):
    rows, width = att.shape
    early, groups, part = w1a.shape[:3]
    late = 4 - early
    fc = width // 2
    pad = (rows // 2 + 15) // 16 * 16
    keep = lambda s: pl.BlockSpec(s, lambda j: (0,) * len(s), pipeline_mode=pl.Buffered(1))
    full = lambda s: pl.BlockSpec(s, lambda j: (0,) * len(s))
    hbm = pl.BlockSpec(memory_space=pltpu.HBM)
    sd = jax.ShapeDtypeStruct
    vm = lambda s, t=BF: pltpu.VMEM(s, t)
    dma = pltpu.SemaphoreType.DMA
    units = len(MLP_STARTS)
    scratch = [
        vm((rows, width), F32), vm((2, pad, width)), vm((rows, width), F32),
        vm((rows, width)), vm((width, rows)), vm((rows, width)), vm((rows, width), F32), vm((rows, width), F32),
        vm((2, groups, part, fc)), vm((2, groups // 2, part, width)), vm((2, groups, part, fc)), vm((2, groups // 2, part, width)),
        vm((2, 4, part, width)), dma((2, 2)), dma((2, 2)), dma((4,)),
    ]
    scratch += gather_scratch(1) * (2 * late)
    for _ in range(units):
        scratch += chip_scratch(part, width, 1, BF)
    quarters = lambda n: sd((n, groups, part, width), BF)
    return pl.pallas_call(
        functools.partial(mlp_kernel, MLP_STARTS), grid=(8,),
        in_specs=[keep((rows, width)), keep((rows, width)), keep(cot.shape), keep((rows, 128)), keep(vec.shape), keep((width, width)),
            hbm, hbm, hbm, hbm],
        out_specs=[hbm] * 4 + [full((groups, 16, part))] + [hbm] * 4 + [full((part, width))] * units,
        out_shape=[sd((2, pad, width), BF), sd((rows, width), F32), sd((rows, width), BF), sd((2, groups // 2, part, width), BF),
            sd((groups, 16, part), F32), quarters(late), quarters(late), quarters(4), quarters(4)] + [sd((part, width), BF)] * units,
        scratch_shapes=scratch,
        compiler_params=pltpu.CompilerParams(vmem_limit_bytes=63 * 2**20, collective_id=6, has_side_effects=True), name="mlp",
    )(att, x, cot, mask, vec, wp, w1a, w2a, w1_own, w2_own)


def att_bwd_kernel(begun, left, q_ref, ko_ref, kp_ref, vo_ref, vp_ref, bias_ref, st_ref, do_ref, o_ref, mixed_ref, dwp, dw1, dw2, small, *rest):
    step = pl.program_id(0)
    last = pl.num_programs(0) - 1
    rows = q_ref.shape[0]
    f, z, mate, da, db = places()
    sources = [dwp] + [w.at[i] for i in range(4) for w in (dw1, dw2)][begun:]
    units = len(sources)
    tots, rest = rest[:begun], rest[begun:]
    dqkv_ref, got_ref, back_ref, small_out = rest[:4]
    outs, rest = rest[4:4 + begun + units], rest[4 + begun + units:]
    kbuf, vbuf, qx, dox, dkv, mine, kv_send, kv_recv, relay_sems = rest[:9]
    scratch = list(rest[9:])

    def take(n):
        refs = scratch[:n]
        del scratch[:n]
        return refs

    every = []
    starts = []
    for i in range(begun):
        every += [[None] * 3 + line_steps(tots[i], outs[i], take(LINE_REFS), [(0, tots[i].shape[0])])[0]]
        starts.append(BWD_LINE + i)
    for i in range(units):
        src = sources[i]
        out = outs[begun + i]
        rows_out = [(0, out.shape[0])]
        if i < units - left:
            every += reduce_steps(src, out, take(REDUCE_REFS), rows_out, mine.at[i % 3])
        else:
            every += chip_steps(src, out, take(CHIP_REFS), rows_out, mine.at[i % 3])
        starts.append(BWD_PACE * i)
    every += reduce_steps(small, small_out, take(REDUCE_REFS), [(0, small_out.shape[0])])
    starts.append(7)
    table = timetable(starts, BWD_TIMES, every)
    relay_start, relay_wait = relay_steps(mixed_ref, back_ref, relay_sems)

    def give(i):
        cols = pl.ds(i * 128 if isinstance(i, int) else pl.multiple_of(i * 128, 128), 128)
        return pltpu.make_async_remote_copy(
            src_ref=dkv.at[i % 2, :, pl.ds(rows, rows)], dst_ref=got_ref.at[:, :, cols],
            send_sem=kv_send.at[i % 2], recv_sem=kv_recv.at[i], device_id=(mate, z), device_id_type=MESH)

    @pl.when(step == 0)
    def _():
        greet(True)
        run_steps(every, table, -9, 0)
        relay_start()
        kbuf[:, 128:] = bias_ref[...]
        lane = lax.broadcasted_iota(jnp.int32, (2 * rows, 128), 1)
        vbuf[:, 128:] = (lane < 3).astype(BF)

    def hook(half):
        for at in range(8):
            @pl.when(step == at)
            def _(at=at):
                run_steps(every, table, 2 * at + half, 2 * at + half + 1)

    @pl.when(step >= 2)
    def _():
        give(step - 2).wait_send()

    hook(0)
    kbuf[:rows, :128] = ko_ref[0]
    kbuf[rows:, :128] = kp_ref[0]
    vbuf[:rows, :128] = vo_ref[0]
    vbuf[rows:, :128] = vp_ref[0]
    lane = lax.broadcasted_iota(jnp.int32, (rows, 128), 1)
    low = lane < 64
    q = q_ref[...]
    do = do_ref[...]
    prod = do.astype(F32) * o_ref[...].astype(F32)
    for h in range(2):
        keep = low if h == 0 else jnp.logical_not(low)
        qx[h, :, :128] = jnp.where(keep, q, jnp.zeros_like(q))
        qx[h, :, 128:] = st_ref[h]
        dox[h, :, :128] = jnp.where(keep, do, jnp.zeros_like(do))
        total = -jnp.sum(jnp.where(keep, prod, 0.0), axis=-1, keepdims=True)
        hi = total.astype(BF).astype(F32)
        mid = (total - hi).astype(BF).astype(F32)
        lo = total - hi - mid
        piece = jnp.where(lane == 0, hi, jnp.where(lane == 1, mid, jnp.where(lane == 2, lo, 0.0)))
        dox[h, :, 128:] = piece.astype(BF)
    dqs = [None, None]
    for part in range(2):
        if part == 1:
            hook(1)
        start = part * rows
        dk = None
        dv = None
        kb = kbuf[start:start + rows, :]
        vb = vbuf[start:start + rows, :]
        for h in range(2):
            s = dotf(kb, qx[h], NT)
            dp = dotf(vb, dox[h], NT)
            p = jnp.exp(s)
            ds = (p * dp).astype(BF)
            p_low = p.astype(BF)
            dv_h = dotf(p_low, dox[h, :, :128], NN)
            dk_h = dotf(ds, qx[h, :, :128], NN)
            dv = dv_h if dv is None else dv + dv_h
            dk = dk_h if dk is None else dk + dk_h
            dq_h = dotf(kb[:, :128], ds, TN)
            dqs[h] = dq_h if dqs[h] is None else dqs[h] + dq_h
        dkv[step % 2, 0, start:start + rows, :] = dk.astype(BF)
        dkv[step % 2, 1, start:start + rows, :] = dv.astype(BF)
    dqs = [d.T for d in dqs]
    dqkv_ref[0] = (jnp.where(low, dqs[0], dqs[1]) * 0.125).astype(BF)
    dqkv_ref[1] = dkv[step % 2, 0, :rows, :]
    dqkv_ref[2] = dkv[step % 2, 1, :rows, :]
    give(step).start()

    @pl.when(step == last)
    def _():
        run_steps(every, table, 16, FOREVER)
        give(step - 1).wait_send()
        give(step).wait_send()
        for i in range(kv_recv.shape[0]):
            give(i).wait_recv()
        relay_wait()


BWD_PACE = 2.5
BWD_LINE = 3
BWD_TIMES = (-2, 1, 3, 6, 8, 10, 12)


def att_bwd(q, kv_own, kv_other, bias, st, do, o, mixed, dwp, dw1, dw2, small, tots, left):
    rows, width = q.shape
    pairs = width // 128
    blk = pl.BlockSpec((rows, 128), lambda i: (0, i))
    key = pl.BlockSpec((1, rows, 128), lambda i: (0, 0, i))
    val = pl.BlockSpec((1, rows, 128), lambda i: (1, 0, i))
    hbm = pl.BlockSpec(memory_space=pltpu.HBM)
    part = dw1.shape[2]
    units = 9 - len(tots)
    scratch = []
    for _ in tots:
        scratch += line_scratch(part, width, 1, BF)
    for i in range(units):
        scratch += (reduce_scratch if i < units - left else chip_scratch)(part, width, 1, BF)
    scratch += reduce_scratch(small.shape[1], small.shape[2], 1, F32)
    whole = lambda s: pl.BlockSpec(s, lambda i: (0,) * len(s))
    return pl.pallas_call(
        functools.partial(att_bwd_kernel, len(tots), left),
        grid=(pairs,),
        in_specs=[blk, key, key, val, val,
            pl.BlockSpec((2 * rows, 128), lambda i: (0, 0)),
            pl.BlockSpec((2, rows, 128), lambda i: (i, 0, 0)), blk, blk, hbm, hbm, hbm, hbm, whole(small.shape)] + [whole((part, width))] * len(tots),
        out_specs=[pl.BlockSpec((3, rows, 128), lambda i: (0, 0, i)), hbm, hbm, whole(small.shape[1:])] + [whole((part, width))] * (units + len(tots)),
        out_shape=[jax.ShapeDtypeStruct((3, rows, width), BF), jax.ShapeDtypeStruct((2, rows, width), BF), jax.ShapeDtypeStruct(mixed.shape, BF)]
        + [jax.ShapeDtypeStruct(small.shape[1:], F32)] + [jax.ShapeDtypeStruct((part, width), BF)] * (units + len(tots)),
        scratch_shapes=[pltpu.VMEM((2 * rows, 256), BF), pltpu.VMEM((2 * rows, 256), BF),
            pltpu.VMEM((2, rows, 256), BF), pltpu.VMEM((2, rows, 256), BF), pltpu.VMEM((2, 2, 2 * rows, 128), BF), pltpu.VMEM((3, 4, part, width), BF),
            pltpu.SemaphoreType.DMA((2,)), pltpu.SemaphoreType.DMA((pairs,)), pltpu.SemaphoreType.DMA((4,))] + scratch,
        compiler_params=pltpu.CompilerParams(vmem_limit_bytes=62 * 2**20, collective_id=1, has_side_effects=True),
        name="att_bwd",
    )(q, kv_own, kv_other, kv_own, kv_other, bias, st, do, o, mixed, dwp, dw1, dw2, small, *tots)


def qback_kernel(half, left, dy_ref, got_ref, x_ref, nt_ref, gmid_ref, vec_ref, w_ref, *rest):
    tots, rest = rest[:left], rest[left:]
    back_ref, rq, rs = rest[:3]
    ends = rest[3:3 + left]
    gn, dw, gx, small, relay_sems = rest[3 + left:8 + left]
    scratch = rest[8 + left:]
    step = pl.program_id(0)
    groups, part = dw.shape[1:3]
    every = []
    for i in range(4):
        refs = scratch[REDUCE_REFS * i:REDUCE_REFS * (i + 1)]
        if i < 3:
            every += reduce_steps(dw.at[i], rq.at[i], refs, even_cuts(part, QBACK_PARTS))
        else:
            every += reduce_steps(small, rs, refs, [(0, small.shape[1])])
    starts = [0, 3, 6, 7]
    scratch = scratch[REDUCE_REFS * 4:]
    for i in range(left):
        line = line_steps(tots[i], ends[i], scratch[LINE_REFS * i:LINE_REFS * (i + 1)], [(0, part)])[0]
        every.append([None] * 3 + line)
        starts.append(QBACK_LINE + i)
    tail = len(every) - left - 1
    table = timetable(starts, QBACK_TIMES, every)
    relay_start, relay_wait = relay_steps(gx, back_ref, relay_sems)

    def put(row, v):
        for i in range(groups):
            small[i, row:row + 1, :] = v[:, i * part:(i + 1) * part]

    col = lambda v: jnp.sum(v, axis=0, keepdims=True)

    @pl.when(step == 0)
    def _():
        greet(True)
        run_steps(every, table, -9, 0)
        gn[...] = jnp.zeros_like(gn)
        small[...] = jnp.zeros_like(small)

    def do(i, y):
        dw[i] = dotf(nt_ref[...], y, NN).astype(BF).reshape(dw.shape[1:])
        every[i][0]()
        gn[...] += dotf(y, w_ref[...], NT)

    @pl.when(step == 0)
    def _():
        y = dy_ref[0]
        put(0, col(y.astype(F32)))
        do(0, y)
        run_steps(every, table, 0, 1)

    @pl.when(step == 1)
    def _():
        do(1, (dy_ref[0].astype(F32) + got_ref[0].astype(F32)).astype(BF))
        run_steps(every, table, 1, 3)

    @pl.when(step == 2)
    def _():
        y = (dy_ref[0].astype(F32) + got_ref[0].astype(F32)).astype(BF)
        put(1, col(y.astype(F32)))
        do(2, y)
        run_steps(every, table, 3, 6)
        z, r = norm_parts(x_ref[...].astype(F32))
        g = gn[...]
        put(2, col(g * z))
        put(3, col(g))
        every[tail][0]()
        res = gmid_ref[...] + norm_back(z, r, g, vec_ref[0:1, :])
        gx[0, :half] = res[:half].astype(BF)
        gx[1, :half] = res[half:].astype(BF)
        gx[:, half:] = jnp.zeros_like(gx[:, half:])
        relay_start()
        run_steps(every, table, 6, FOREVER)
        relay_wait()


LEFT = 5
QBACK_PARTS = 1
QBACK_LINE = -6
QBACK_TIMES = (None, 1, 3, 5, 7, 9, 11)


def qback(dy, got, x, nt, gmid, vec, w, groups, tots):
    rows, width = x.shape
    part = width // groups
    once = pl.Buffered(1)
    full = lambda s: pl.BlockSpec(s, lambda j: (0,) * len(s))
    keep = lambda s: pl.BlockSpec(s, lambda j: (0,) * len(s), pipeline_mode=once)
    hbm = pl.BlockSpec(memory_space=pltpu.HBM)
    sd = jax.ShapeDtypeStruct
    scratch = []
    for _ in range(3):
        scratch += reduce_scratch(part, width, QBACK_PARTS, BF)
    scratch += reduce_scratch(8, part, 1, F32)
    for _ in tots:
        scratch += line_scratch(part, width, 1, BF)
    pad = (rows // 2 + 15) // 16 * 16
    return pl.pallas_call(functools.partial(qback_kernel, rows // 2, len(tots)), grid=(3,),
        in_specs=[pl.BlockSpec((1, rows, width), lambda j: (j, 0, 0)), pl.BlockSpec((1, rows, width), lambda j: (jnp.maximum(j - 1, 0), 0, 0)),
            keep((rows, width)), keep((width, rows)), keep((rows, width)), full(vec.shape), pl.BlockSpec((width, width), lambda j: (0, j))] + [keep((part, width))] * len(tots),
        out_specs=[hbm, full((3, part, width)), full((8, part))] + [full((part, width))] * len(tots),
        out_shape=[sd((2, pad, width), BF), sd((3, part, width), BF), sd((8, part), F32)] + [sd((part, width), BF)] * len(tots),
        scratch_shapes=[pltpu.VMEM((rows, width), F32), pltpu.VMEM((3, groups, part, width), BF),
            pltpu.VMEM((2, pad, width), BF), pltpu.VMEM((groups, 8, part), F32),
            pltpu.SemaphoreType.DMA((4,))] + scratch,
        compiler_params=pltpu.CompilerParams(vmem_limit_bytes=63 * 2**20, collective_id=2, has_side_effects=True), name="qback")(
            dy, got, x, nt, gmid, vec, w, *tots)


def fast_device(
    tokens,
    valid_len,
    cotangent,
    norm1_gain,
    norm1_shift,
    qkv_weight,
    query_bias,
    value_bias,
    proj_weight,
    proj_bias,
    attn_scale,
    norm2_gain,
    norm2_shift,
    fc1_weight,
    fc1_bias,
    fc2_weight,
    fc2_bias,
    mlp_scale,
):
    groups = lax.axis_size("fsdp")
    images_here, tok_here, width = tokens.shape
    part = width // groups
    rows = 2 * tok_here
    vectors = jnp.concatenate(
        [
            norm1_gain, norm1_shift, query_bias, value_bias, proj_bias, attn_scale, norm2_gain, norm2_shift,
            fc2_bias, mlp_scale, fc1_bias,
        ]
    )
    small = jnp.concatenate([vectors.astype(F32), valid_len.astype(F32), jnp.zeros((2 * part - images_here,), F32)])
    x, normed_t, q, kv, kv_other, wq, wp, vec, mask, w1_cut = qkv(
        tokens, small.reshape(16, part), qkv_weight, proj_weight, fc1_weight, groups
    )
    wq, wp = wq.reshape(width, -1), wp.reshape(width, width)
    attended, stats, cot, w1, w2 = att_fwd(q, kv, kv_other, mask, FWD_BLOCKS(rows), cotangent, w1_cut, fc2_weight, groups)
    mixed, grad_mid, grad_att, dwp, small2, _w1, _w2, dw1, dw2, *first_sums = mlp(
        attended, x, cot, mask, vec, wp, w1, w2, w1_cut, fc2_weight
    )
    dqkv, got, mixed_out, sums2, *later_sums = att_bwd(
        q, kv, kv_other, mask, stats, grad_att, attended, mixed, dwp.reshape(groups, part, width), dw1, dw2, small2,
        first_sums, LEFT,
    )
    grad_x, total_q, sums1, *last_sums = qback(dqkv, got, x, normed_t, grad_mid, vec, wq, groups, later_sums[-LEFT:])
    quarters = later_sums[:-LEFT] + last_sums
    total_p = quarters.pop(len(first_sums))
    total_1 = jnp.stack([v.reshape(part, groups, -1) for v in quarters[0::2]], axis=2).reshape(part, -1)
    total_2 = jnp.concatenate(quarters[1::2], axis=0)
    total_q = jnp.concatenate([total_q[0], total_q[1], total_q[2]], axis=1).astype(F32)
    squares = sums2[14, : images_here * 5].reshape(images_here, 5)
    rms = jnp.sqrt(squares / (valid_len.astype(F32)[:, None] * width))
    return (
        mixed_out[:, :tok_here], grad_x[:, :tok_here].astype(F32), rms, sums1[2], sums1[3], total_q, sums1[0], sums1[1],
        total_p.astype(F32), sums2[5], sums2[4], sums2[2], sums2[3], total_1.astype(F32), sums2[10:14].reshape(-1),
        total_2.astype(F32), sums2[1], sums2[0],
    )


def FWD_BLOCKS(rows):
    first = (rows // 2 + 15) // 16 * 16
    return (first, rows - first)


def solution(mesh):
    in_specs = (
        P("fsdp", "seq", None),
        P("fsdp"),
        P("fsdp", "seq", None),
        P("fsdp"),
        P("fsdp"),
        P("fsdp", None),
        P("fsdp"),
        P("fsdp"),
        P("fsdp", None),
        P("fsdp"),
        P("fsdp"),
        P("fsdp"),
        P("fsdp"),
        P("fsdp", None),
        P("fsdp"),
        P("fsdp", None),
        P("fsdp"),
        P("fsdp"),
    )
    out_specs = (
        P("fsdp", "seq", None),
        P("fsdp", "seq", None),
        P("fsdp", None),
        P("fsdp"),
        P("fsdp"),
        P("fsdp", None),
        P("fsdp"),
        P("fsdp"),
        P("fsdp", None),
        P("fsdp"),
        P("fsdp"),
        P("fsdp"),
        P("fsdp"),
        P("fsdp", None),
        P("fsdp"),
        P("fsdp", None),
        P("fsdp"),
        P("fsdp"),
    )
    seq_count = mesh.shape["seq"]
    paired = seq_count == 4 and mesh.shape["fsdp"] == 8
    return jax.shard_map(
        fast_device if paired else generic_device, mesh=mesh, in_specs=in_specs, out_specs=out_specs, check_vma=False
    )
```
